32 devices in a mesh: group: 4 (over x, core), sub: 8 (over z, y).
Axes of the slice: x: 2, y: 2, z: 4, core: 2. Of those that a mesh axis runs over, the one named last changes fastest.
Arguments:
- users: float32 [32768, 512], P(('group', 'sub')), may hold values from -1.2 to 1.2
- items: float32 [2048, 512], P(('group', 'sub')), may hold values from -1.2 to 1.2
- ratings: bfloat16 [4, 32768, 512], P(None, ('group', 'sub')), may hold values from -5 to 5
- occupancy: int32 [4, 256, 4], P(None, ('group', 'sub')), may hold values 0 or 1
Outputs:
- users_out: float32 [32768, 512], P(('group', 'sub'))
- items_out: float32 [2048, 512], P(('group', 'sub'))
The draws below stay inside these ranges and needn't reach their ends.
All inputs are finite; a program needn't handle non-finite values. No bound on the sum of `occupancy` on one device may be relied on, other than what follows from the above.
Results may differ from the reference program's by a relative error of at most 0.0003.
Values sent between devices are 32-bit elements; how exact they have to be, the bound alone decides.
No kernel may reach another device: no remote copies, remote signals or barrier semaphores. Data moves between devices by JAX's collectives and lax.ppermute only.
A program may use at most 64 MiB of HBM per device.

```python
import jax
import jax.numpy as jnp
from jax import lax

RANK = 512
TILE = 128
ITEM_BLOCK = 512
USERS_DEV = 1024
STRATA = 4
USERS = 32768
ITEMS = 2048
N_GROUP = 4
N_SUB = 8


def set_ends(result, own_key, least, top_value):
    spot = [jax.random.randint(jax.random.fold_in(own_key, axis), (), 0, length) for axis, length in enumerate(result.shape)]
    main_axis = result.shape.index(max(result.shape))
    next_to = spot[:main_axis] + [(spot[main_axis] + 1) % result.shape[main_axis]] + spot[main_axis + 1:]
    return result.at[tuple(spot)].set(least).at[tuple(next_to)].set(top_value)


def levels(stream_key, dims, cuts, least, high):
    def one(axis_at, parts):
        steps = jax.random.uniform(jax.random.fold_in(jax.random.fold_in(stream_key, 6), axis_at), (parts,), jnp.float32, least / len(cuts), high / len(cuts))
        return jnp.repeat(jnp.exp(steps), dims[axis_at] // parts).reshape((-1,) + (1,) * (len(dims) - axis_at - 1))

    factor_of = one(*cuts[0])
    for cut in cuts[1:]:
        factor_of = factor_of * one(*cut)
    return factor_of


def normal_values(own_key, extent, deviation, most, shards=(), held_as=jnp.bfloat16):
    drawn = jax.random.normal(own_key, extent, jnp.float32) * deviation
    if len(shards) > 0:
        drawn = levels(own_key, extent, shards, -0.22, 0.18) * drawn
    return jnp.clip(drawn, min=-most, max=most).astype(held_as)


def setup_inputs(seed: int = 0) -> dict:
    key_of = jax.random.split(jax.random.key(seed), 5)
    return {
        "users": normal_values(key_of[0], (USERS, RANK), 0.21, 1.2, ((0, 32),), jnp.float32),
        "items": normal_values(key_of[1], (ITEMS, RANK), 0.21, 1.2, ((0, 32),), jnp.float32),
        "ratings": normal_values(key_of[2], (STRATA, USERS, ITEM_BLOCK), 1.0, 5.0, ((1, 32),)),
        "occupancy": set_ends((jax.random.randint(key_of[3], (STRATA, USERS // TILE, ITEM_BLOCK // TILE), 0, 4) < 1).astype(jnp.int32), jax.random.fold_in(key_of[3], 1), 0, 1),
    }


def expand_mask(occ, rows, cols):
    tiles = occ.astype(jnp.float32)[:, None, :, None]
    tiles = jnp.broadcast_to(tiles, (rows // TILE, TILE, cols // TILE, TILE))
    return tiles.reshape(rows, cols)


def errors(user_rows, block, rate, occ):
    pred = lax.dot_general(user_rows, block, (((1,), (1,)), ((), ())), precision=lax.Precision.HIGHEST, preferred_element_type=jnp.float32)
    mask = expand_mask(occ, user_rows.shape[0], block.shape[0])
    return mask * (rate.astype(jnp.float32) - pred)


def reference(users, items, ratings, occupancy):
    user_blocks = users.reshape(N_GROUP, N_SUB, USERS_DEV, RANK)
    blocks = items.reshape(N_GROUP, ITEM_BLOCK, RANK)
    for section in range(STRATA):
        rate = ratings[section].reshape(N_GROUP, N_SUB, USERS_DEV, ITEM_BLOCK)
        occ = occupancy[section].reshape(N_GROUP, N_SUB, USERS_DEV // TILE, ITEM_BLOCK // TILE)

        def one_group(packed):
            group_users, block, group_rate, group_occ = packed

            def one_sub(inner):
                user_rows, sub_rate, sub_occ = inner
                err = errors(user_rows, block, sub_rate, sub_occ)
                pull = jnp.dot(err, block, precision=lax.Precision.HIGHEST, preferred_element_type=jnp.float32)
                new_rows = user_rows + 0.02 * (pull - 0.05 * user_rows)
                term = lax.dot_general(err, user_rows, (((0,), (0,)), ((), ())), precision=lax.Precision.HIGHEST, preferred_element_type=jnp.float32)
                return new_rows, term

            new_users, terms = lax.map(one_sub, (group_users, group_rate, group_occ))
            grad = jnp.sum(terms, axis=0)
            return new_users, block + 0.005 * (grad - 0.05 * block)

        user_blocks, blocks = lax.map(one_group, (user_blocks, blocks, rate, occ))
        blocks = jnp.roll(blocks, 1, axis=0)
    return user_blocks.reshape(USERS, RANK), blocks.reshape(ITEMS, RANK)
```

```python
import functools

import jax
import jax.numpy as jnp
from jax import lax
from jax.experimental import pallas as pl
from jax.experimental.pallas import tpu as pltpu
from jax.sharding import PartitionSpec as P

TILE = 128
CHUNKS = 2
BLOCK = 256
ANY = pl.BlockSpec(memory_space=pltpu.VMEM)
SMEM = pl.BlockSpec(memory_space=pltpu.SMEM)
F32 = jnp.float32
BF16 = jnp.bfloat16


def split(x):
    hi = x.astype(BF16)
    return hi, (x - hi.astype(F32)).astype(BF16)


def dot3(a, b, dims):
    (ah, al), (bh, bl) = a, b
    dot = functools.partial(lax.dot_general, dimension_numbers=(dims, ((), ())), preferred_element_type=F32)
    return dot(ah, bh) + (dot(ah, bl) + dot(al, bh))


def params(mib):
    return pltpu.CompilerParams(vmem_limit_bytes=mib * 1024 * 1024)


def grad_kernel(ny, first_tile, stratum, out_q, *refs):
    where, occ, users, rate = refs[:4]
    pieces = refs[4:4 + ny]
    err_hi, err_lo, v_hi, v_lo = refs[4 + ny:8 + ny]
    grads = refs[8 + ny:8 + 2 * ny]
    block, total = refs[8 + 2 * ny:]
    step = pl.program_id(0)
    mine = where[0]
    rows, rank = total.shape

    @pl.when(step == 0)
    def _():
        for r in range(ny):
            block[:, mine ^ r] = pieces[r][...]
        hi, lo = split(block[...].reshape(rows, rank))
        v_hi[...] = hi
        v_lo[...] = lo

    u = split(users[...])
    pred = dot3(u, (v_hi[...], v_lo[...]), ((1,), (1,)))
    err = rate[...].reshape(pred.shape).astype(F32) - pred
    tiles = err.shape[0] // TILE
    parts = []
    for a in range(tiles):
        line = []
        for b in range(rows // TILE):
            seen = occ[stratum, step * tiles + a, first_tile + b]
            part = err[a * TILE:(a + 1) * TILE, b * TILE:(b + 1) * TILE]
            line.append(jnp.where(seen == 1, part, 0.0))
        parts.append(jnp.concatenate(line, axis=1))
    e = split(jnp.concatenate(parts, axis=0))
    err_hi[...], err_lo[...] = e
    term = dot3(e, u, ((0,), (0,)))

    @pl.when(step == 0)
    def _():
        total[...] = term

    @pl.when(step > 0)
    def _():
        total[...] += term

    @pl.when(step == pl.num_programs(0) - 1)
    def _():
        block[...] = total[...].reshape(block.shape)
        view = block if out_q == block.shape[2] else None
        if view is not None:
            for r in range(ny):
                grads[r][...] = block[:, mine ^ r]
        else:
            whole = total[...].reshape(-1, ny, out_q, rank)
            for r in range(ny):
                for y in range(ny):
                    @pl.when((mine ^ r) == y)
                    def _():
                        grads[r][...] = whole[:, y]


def gradients(where, occ, users, ratings, pieces, stratum, chunk, out_q):
    ny = len(pieces)
    nz, q, rank = pieces[0].shape
    rows = nz * ny * q
    n_users = users.shape[0]
    full = lambda shape: pl.BlockSpec(shape, lambda i: (0,) * len(shape))
    gshape = (rows // (ny * out_q), out_q, rank)
    return pl.pallas_call(
        functools.partial(grad_kernel, ny, chunk * rows // TILE, stratum, out_q),
        grid=(n_users // BLOCK,),
        in_specs=[SMEM, SMEM, pl.BlockSpec((BLOCK, rank), lambda i: (i, 0)),
                  pl.BlockSpec((1, BLOCK, rows), lambda i: (stratum, i, chunk))] + [full(p.shape) for p in pieces],
        out_specs=[pl.BlockSpec((BLOCK, rows), lambda i: (i, 0))] * 2 + [full((rows, rank))] * 2 + [full(gshape)] * ny,
        out_shape=[jax.ShapeDtypeStruct((n_users, rows), BF16)] * 2 + [jax.ShapeDtypeStruct((rows, rank), BF16)] * 2
        + [jax.ShapeDtypeStruct(gshape, F32)] * ny,
        scratch_shapes=[pltpu.VMEM((nz, ny, q, rank), F32), pltpu.VMEM((rows, rank), F32)],
        compiler_params=params(28),
        cost_estimate=pl.CostEstimate(flops=12 * n_users * rows * rank, bytes_accessed=4 * n_users * rank, transcendentals=0),
        name="gradients",
    )(where, occ, users, ratings, *pieces)


def step_kernel(n, *refs):
    users, out = refs[0], refs[-1]
    pull = None
    for i in range(n):
        eh, el, vh, vl = refs[1 + 4 * i:5 + 4 * i]
        part = dot3((eh[...], el[...]), (vh[...], vl[...]), ((1,), (0,)))
        pull = part if pull is None else pull + part
    u = users[...]
    out[...] = u + 0.02 * (pull - 0.05 * u)


def user_step(users, parts):
    n_users, rank = users.shape
    specs, flat = [], []
    for eh, el, vh, vl in parts:
        flat += [eh, el, vh, vl]
        specs += [pl.BlockSpec((BLOCK, eh.shape[1]), lambda i: (i, 0))] * 2 + [pl.BlockSpec(vh.shape, lambda i: (0, 0))] * 2
    rows = sum(p[2].shape[0] for p in parts)
    own = pl.BlockSpec((BLOCK, rank), lambda i: (i, 0))
    return pl.pallas_call(
        functools.partial(step_kernel, len(parts)),
        grid=(n_users // BLOCK,),
        in_specs=[own] + specs,
        out_specs=own,
        out_shape=jax.ShapeDtypeStruct(users.shape, F32),
        compiler_params=params(28),
        cost_estimate=pl.CostEstimate(flops=6 * n_users * rows * rank, bytes_accessed=8 * n_users * rank, transcendentals=0),
        name="user_step",
    )(users, *flat)


def cut_kernel(ny, nz, *refs):
    where = refs[0]
    terms, outs = refs[1:1 + ny], refs[1 + ny:]
    z = where[1]
    for r in range(nz):
        total = terms[0][z ^ r]
        for t in terms[1:]:
            total = total + t[z ^ r]
        outs[r][...] = total


def cut(where, terms):
    nz, q, rank = terms[0].shape
    return pl.pallas_call(
        functools.partial(cut_kernel, len(terms), nz),
        in_specs=[SMEM] + [ANY] * len(terms),
        out_specs=[ANY] * nz,
        out_shape=[jax.ShapeDtypeStruct((q, rank), F32)] * nz,
        compiler_params=params(8),
        name="cut",
    )(where, *terms)


def join_kernel(nz, *refs):
    where, pieces, out = refs[0], refs[1:-1], refs[-1]
    for r in range(nz):
        out[where[1] ^ r] = pieces[r][...]


def join(where, pieces):
    nz = len(pieces)
    return pl.pallas_call(
        functools.partial(join_kernel, nz),
        in_specs=[SMEM] + [ANY] * nz,
        out_specs=ANY,
        out_shape=jax.ShapeDtypeStruct((nz,) + pieces[0].shape, F32),
        compiler_params=params(8),
        name="join",
    )(where, *pieces)


def new_rows(old, terms):
    total = functools.reduce(jnp.add, terms)
    return old + 0.005 * (total - 0.05 * old)


def per_device(n_group, n_sub, users, items, ratings, occupancy):
    strata = ratings.shape[0]
    share, rank = items.shape
    ny = 1
    while ny * ny * 2 <= n_sub:
        ny *= 2
    nz = n_sub // ny
    chunks = max(1, min(CHUNKS, share // 16))
    k = lax.axis_index("sub")
    where = jnp.stack([k % ny, k // ny]).astype(jnp.int32)

    def over_y(x, r):
        return lax.ppermute(x, "sub", [(i, i ^ r) for i in range(n_sub)])

    def over_z(x, r):
        return lax.ppermute(x, "sub", [(i, i ^ (r * ny)) for i in range(n_sub)])

    def onward(x, r):
        route = []
        for g in range(n_group):
            for i in range(n_sub):
                route.append((g * n_sub + i, (g + 1) % n_group * n_sub + (i ^ (r * ny))))
        return lax.ppermute(x, ("group", "sub"), route)

    q = share // chunks
    own = join(where, [items] + [over_z(items, r) for r in range(1, nz)])
    owns = [own] + [over_y(own, r) for r in range(1, ny)]
    if chunks == 1:
        pieces = [owns]
        olds = [items]
    else:
        order = jnp.stack([owns[r] for r in range(ny)])
        order = order if ny == 1 else jnp.take(order, jnp.arange(ny) ^ where[0], axis=0)
        block = order.transpose(1, 0, 2, 3).reshape(chunks, nz, ny, q, rank)
        pieces = [[jnp.take(block[c], where[0] ^ r, axis=1) for r in range(ny)] for c in range(chunks)]
        olds = [jnp.take(pieces[c][0], where[1], axis=0) for c in range(chunks)]

    for s in range(strata):
        last = s == strata - 1
        parts, grads = [], []
        for c in range(chunks):
            res = gradients(where, occupancy, users, ratings, pieces[c], s, c, share if last else q)
            parts.append(res[:4])
            grads.append([res[4]] + [over_y(res[4 + r], r) for r in range(1, ny)])
        new_users = user_step(users, parts)
        if last:
            terms = [jnp.concatenate([g[r] for g in grads]) if chunks > 1 else grads[0][r] for r in range(ny)]
            cuts = cut(where, terms)
            old = olds[0]
            if chunks > 1:
                mine = [jnp.take(v, where[0], axis=1) for v in lasts(pieces, where, share)]
                old = jnp.take(jnp.concatenate(mine), where[1], axis=0)
            rows = new_rows(old, [cuts[0]] + [over_z(cuts[r], r) for r in range(1, nz)])
            rows = lax.ppermute(rows, "group", [(g, (g + 1) % n_group) for g in range(n_group)])
            return new_users, rows
        for c in range(chunks):
            cuts = cut(where, grads[c])
            rows = new_rows(olds[c], [cuts[0]] + [over_z(cuts[r], r) for r in range(1, nz)])
            moved = [onward(rows, r) for r in range(nz)]
            olds[c] = moved[0]
            own = join(where, moved)
            pieces[c] = [own] + [over_y(own, r) for r in range(1, ny)]
        users = new_users


def lasts(pieces, where, share):
    out = []
    for p in pieces:
        ny = len(p)
        nz, q, rank = p[0].shape
        order = jnp.take(jnp.stack(p), jnp.arange(ny) ^ where[0], axis=0)
        out.append(order.transpose(1, 0, 2, 3).reshape(-1, ny, share, rank))
    return out


def solution(mesh):
    spec = P(("group", "sub"), None)
    third = P(None, ("group", "sub"), None)
    return jax.shard_map(
        functools.partial(per_device, mesh.shape["group"], mesh.shape["sub"]),
        mesh=mesh,
        in_specs=(spec, spec, third, third),
        out_specs=(spec, spec),
        check_vma=False,
    )
```

```python
import functools

import jax
import jax.numpy as jnp
from jax import lax
from jax.experimental import pallas as pl
from jax.experimental.pallas import tpu as pltpu
from jax.sharding import PartitionSpec as P

TILE = 128
CHUNKS = 2
BLOCK = 512
VMEM = pl.BlockSpec(memory_space=pltpu.VMEM)
SMEM = pl.BlockSpec(memory_space=pltpu.SMEM)
F32 = jnp.float32
BF16 = jnp.bfloat16


def split(x):
    hi = x.astype(BF16)
    return hi, (x - hi.astype(F32)).astype(BF16)


def dot3(a, b, dims):
    (ah, al), (bh, bl) = a, b
    dot = functools.partial(lax.dot_general, dimension_numbers=(dims, ((), ())), preferred_element_type=F32)
    return dot(ah, bh) + (dot(ah, bl) + dot(al, bh))


def params(mib):
    return pltpu.CompilerParams(vmem_limit_bytes=mib * 1024 * 1024)


def grad_kernel(ny, chunk, stratum, *refs):
    where, occ, users, rate = refs[:4]
    pieces = refs[4:4 + ny]
    err_hi, err_lo, v_hi, v_lo, old = refs[4 + ny:9 + ny]
    grads = refs[9 + ny:9 + 2 * ny]
    block, total, vt_hi, vt_lo = refs[9 + 2 * ny:]
    mine = where[0]
    rows, rank = total.shape
    steps, q_in, _ = pieces[0].shape
    for r in range(ny):
        for z in range(steps):
            block[pl.ds((z * ny + (mine ^ r)) * q_in, q_in), :] = pieces[r][z]
    v = block[...]
    v_hi[...], v_lo[...] = split(v)
    vt_hi[...], vt_lo[...] = split(v.T)
    cut, q, _ = grads[0].shape
    old[...] = block[pl.ds((lax.rem(where[1], cut) * ny + mine) * q, q), :]
    for first in range(0, users.shape[0], BLOCK):
        at = slice(first, first + BLOCK)
        u = split(users[at, :])
        pred = dot3(u, (vt_hi[...], vt_lo[...]), ((1,), (0,)))
        err = rate[stratum, at, chunk * rows:(chunk + 1) * rows].astype(F32) - pred
        parts = []
        for a in range(BLOCK // TILE):
            line = []
            for b in range(rows // TILE):
                seen = occ[stratum, first // TILE + a, chunk * rows // TILE + b]
                part = err[a * TILE:(a + 1) * TILE, b * TILE:(b + 1) * TILE]
                line.append(jnp.where(seen == 1, part, 0.0))
            parts.append(jnp.concatenate(line, axis=1))
        err = jnp.concatenate(parts, axis=0)
        err_hi[at, :], err_lo[at, :] = split(err)
        term = dot3(split(err.T), u, ((1,), (0,)))
        if first == 0:
            total[...] = term
        else:
            total[...] += term
    for r in range(ny):
        for z in range(cut):
            grads[r][z] = total[pl.ds((z * ny + (mine ^ r)) * q, q), :]


def gradients(where, occ, users, ratings, pieces, stratum, chunk, q):
    ny = len(pieces)
    steps, q_in, rank = pieces[0].shape
    rows = steps * ny * q_in
    n_users = users.shape[0]
    gshape = (rows // (ny * q), q, rank)
    return pl.pallas_call(
        functools.partial(grad_kernel, ny, chunk, stratum),
        in_specs=[SMEM, SMEM] + [VMEM] * (2 + ny),
        out_specs=[VMEM] * (5 + ny),
        out_shape=[jax.ShapeDtypeStruct((n_users, rows), BF16)] * 2 + [jax.ShapeDtypeStruct((rows, rank), BF16)] * 2
        + [jax.ShapeDtypeStruct((q, rank), F32)] + [jax.ShapeDtypeStruct(gshape, F32)] * ny,
        scratch_shapes=[pltpu.VMEM((rows, rank), F32)] * 2 + [pltpu.VMEM((rank, rows), BF16)] * 2,
        compiler_params=params(24),
        cost_estimate=pl.CostEstimate(flops=12 * n_users * rows * rank, bytes_accessed=4 * n_users * rank, transcendentals=0),
        name="gradients",
    )(where, occ, users, ratings, *pieces)


def step_kernel(n, *refs):
    users, out = refs[0], refs[-1]
    for first in range(0, users.shape[0], BLOCK):
        at = slice(first, first + BLOCK)
        u = users[at, :]
        pull = None
        for i in range(n):
            eh, el, vh, vl = refs[1 + 4 * i:5 + 4 * i]
            part = dot3((eh[at, :], el[at, :]), (vh[...], vl[...]), ((1,), (0,)))
            pull = part if pull is None else pull + part
        out[at, :] = u + 0.02 * (pull - 0.05 * u)


def user_step(users, parts):
    n_users, rank = users.shape
    rows = sum(p[2].shape[0] for p in parts)
    return pl.pallas_call(
        functools.partial(step_kernel, len(parts)),
        in_specs=[VMEM] * (1 + 4 * len(parts)),
        out_specs=VMEM,
        out_shape=jax.ShapeDtypeStruct(users.shape, F32),
        compiler_params=params(24),
        cost_estimate=pl.CostEstimate(flops=6 * n_users * rows * rank, bytes_accessed=8 * n_users * rank, transcendentals=0),
        name="user_step",
    )(users, *[x for p in parts for x in p])


def new_rows(old, terms):
    return old + 0.005 * (jnp.sum(terms, axis=0) - 0.05 * old)


def per_device(n_group, n_sub, users, items, ratings, occupancy):
    strata = ratings.shape[0]
    share, rank = items.shape
    ny = 1
    while ny * ny * 4 <= n_sub:
        ny *= 2
    nz = n_sub // ny
    chunks = max(1, min(CHUNKS, share // 8))
    k = lax.axis_index("sub")
    where = jnp.stack([k % ny, k // ny]).astype(jnp.int32)
    lines = [[z * ny + y for z in range(nz)] for y in range(ny)]

    def over_y(x, r):
        return lax.ppermute(x, "sub", [(i, i ^ r) for i in range(n_sub)])

    def over_z(x):
        return lax.all_to_all(x, "sub", 0, 0, axis_index_groups=lines)

    def gather_z(x):
        return over_z(jnp.broadcast_to(x, (nz,) + x.shape))

    def onward(x, r):
        route = []
        for g in range(n_group):
            for i in range(n_sub):
                route.append((g * n_sub + i, (g + 1) % n_group * n_sub + (i ^ r)))
        return lax.ppermute(x, ("group", "sub"), route)

    q = share // chunks
    own = gather_z(items)
    pieces = []
    for c in range(chunks):
        part = own[c * (nz // chunks):(c + 1) * (nz // chunks)]
        pieces.append([part] + [over_y(part, r) for r in range(1, ny)])

    for s in range(strata):
        last = s == strata - 1
        parts, grads, olds = [], [], []
        for c in range(chunks):
            res = gradients(where, occupancy, users, ratings, pieces[c], s, c, share if last else q)
            parts.append(res[:4])
            olds.append(res[4])
            term = res[5]
            for r in range(1, ny):
                term = term + over_y(res[5 + r], r)
            grads.append(term)
        new_users = user_step(users, parts)
        if last:
            old = olds[0]
            for c in range(1, chunks):
                old = jnp.where(where[1] // (nz // chunks) == c, olds[c], old)
            rows = new_rows(old, over_z(jnp.concatenate(grads)))
            rows = lax.ppermute(rows, "group", [(g, (g + 1) % n_group) for g in range(n_group)])
            return new_users, rows
        for c in range(chunks):
            own = gather_z(new_rows(olds[c], over_z(grads[c])))
            pieces[c] = [onward(own, r) for r in range(ny)]
        users = new_users


def solution(mesh):
    spec = P(("group", "sub"), None)
    third = P(None, ("group", "sub"), None)
    return jax.shard_map(
        functools.partial(per_device, mesh.shape["group"], mesh.shape["sub"]),
        mesh=mesh,
        in_specs=(spec, spec, third, third),
        out_specs=(spec, spec),
        check_vma=False,
    )
```

```python
import functools

import jax
import jax.numpy as jnp
from jax import lax
from jax.experimental import pallas as pl
from jax.experimental.pallas import tpu as pltpu
from jax.sharding import PartitionSpec as P

TILE = 128
CHUNKS = 2
BLOCK = 512
VMEM = pl.BlockSpec(memory_space=pltpu.VMEM)
SMEM = pl.BlockSpec(memory_space=pltpu.SMEM)
F32 = jnp.float32
BF16 = jnp.bfloat16


def split(x):
    hi = x.astype(BF16)
    return hi, (x - hi.astype(F32)).astype(BF16)


def dot3(a, b, dims):
    (ah, al), (bh, bl) = a, b
    dot = functools.partial(lax.dot_general, dimension_numbers=(dims, ((), ())), preferred_element_type=F32)
    return dot(ah, bh) + (dot(ah, bl) + dot(al, bh))


def params(mib):
    return pltpu.CompilerParams(vmem_limit_bytes=mib * 1024 * 1024)


def grad_kernel(ny, chunk, stratum, *refs):
    where, occ, users, rate = refs[:4]
    pieces = refs[4:4 + ny]
    err_hi, err_lo, v_hi, v_lo, old = refs[4 + ny:9 + ny]
    grads = refs[9 + ny:9 + 2 * ny]
    block, total, vt_hi, vt_lo = refs[9 + 2 * ny:]
    mine = where[0]
    rows, rank = total.shape
    steps, q_in, _ = pieces[0].shape
    for r in range(ny):
        for z in range(steps):
            block[pl.ds((z * ny + (mine ^ r)) * q_in, q_in), :] = pieces[r][z]
    v = block[...]
    v_hi[...], v_lo[...] = split(v)
    vt_hi[...], vt_lo[...] = split(v.T)
    cut, q, _ = grads[0].shape
    old[...] = block[pl.ds((lax.rem(where[1], cut) * ny + mine) * q, q), :]
    for first in range(0, users.shape[0], BLOCK):
        at = slice(first, first + BLOCK)
        u = split(users[at, :])
        pred = dot3(u, (vt_hi[...], vt_lo[...]), ((1,), (0,)))
        err = rate[stratum, at, chunk * rows:(chunk + 1) * rows].astype(F32) - pred
        parts = []
        for a in range(BLOCK // TILE):
            line = []
            for b in range(rows // TILE):
                seen = occ[stratum, first // TILE + a, chunk * rows // TILE + b]
                part = err[a * TILE:(a + 1) * TILE, b * TILE:(b + 1) * TILE]
                line.append(jnp.where(seen == 1, part, 0.0))
            parts.append(jnp.concatenate(line, axis=1))
        err = jnp.concatenate(parts, axis=0)
        err_hi[at, :], err_lo[at, :] = split(err)
        term = dot3(split(err.T), u, ((1,), (0,)))
        if first == 0:
            total[...] = term
        else:
            total[...] += term
    for r in range(ny):
        for z in range(cut):
            grads[r][z] = total[pl.ds((z * ny + (mine ^ r)) * q, q), :]


def gradients(where, occ, users, ratings, pieces, stratum, chunk, q):
    ny = len(pieces)
    steps, q_in, rank = pieces[0].shape
    rows = steps * ny * q_in
    n_users = users.shape[0]
    gshape = (rows // (ny * q), q, rank)
    return pl.pallas_call(
        functools.partial(grad_kernel, ny, chunk, stratum),
        in_specs=[SMEM, SMEM] + [VMEM] * (2 + ny),
        out_specs=[VMEM] * (5 + ny),
        out_shape=[jax.ShapeDtypeStruct((n_users, rows), BF16)] * 2 + [jax.ShapeDtypeStruct((rows, rank), BF16)] * 2
        + [jax.ShapeDtypeStruct((q, rank), F32)] + [jax.ShapeDtypeStruct(gshape, F32)] * ny,
        scratch_shapes=[pltpu.VMEM((rows, rank), F32)] * 2 + [pltpu.VMEM((rank, rows), BF16)] * 2,
        compiler_params=params(24),
        cost_estimate=pl.CostEstimate(flops=12 * n_users * rows * rank, bytes_accessed=4 * n_users * rank, transcendentals=0),
        name="gradients",
    )(where, occ, users, ratings, *pieces)


def step_kernel(n, *refs):
    users, out = refs[0], refs[-1]
    for first in range(0, users.shape[0], BLOCK):
        at = slice(first, first + BLOCK)
        u = users[at, :]
        pull = None
        for i in range(n):
            eh, el, vh, vl = refs[1 + 4 * i:5 + 4 * i]
            part = dot3((eh[at, :], el[at, :]), (vh[...], vl[...]), ((1,), (0,)))
            pull = part if pull is None else pull + part
        out[at, :] = u + 0.02 * (pull - 0.05 * u)


def user_step(users, parts):
    n_users, rank = users.shape
    rows = sum(p[2].shape[0] for p in parts)
    return pl.pallas_call(
        functools.partial(step_kernel, len(parts)),
        in_specs=[VMEM] * (1 + 4 * len(parts)),
        out_specs=VMEM,
        out_shape=jax.ShapeDtypeStruct(users.shape, F32),
        compiler_params=params(24),
        cost_estimate=pl.CostEstimate(flops=6 * n_users * rows * rank, bytes_accessed=8 * n_users * rank, transcendentals=0),
        name="user_step",
    )(users, *[x for p in parts for x in p])


def cut_kernel(ny, nz, *refs):
    where, outs = refs[0], refs[-nz:]
    terms = refs[1:-nz]
    chunks = [terms[i:i + ny] for i in range(0, len(terms), ny)]
    each = nz // len(chunks)
    for t in range(nz):
        parts = [x[t % each] for x in chunks[t // each]]
        total = functools.reduce(jnp.add, parts)
        for r in range(nz):
            @pl.when((where[1] ^ t) == r)
            def _():
                outs[r][...] = total


def cut(where, chunks):
    ny = len(chunks[0])
    each, q, rank = chunks[0][0].shape
    nz = each * len(chunks)
    return pl.pallas_call(
        functools.partial(cut_kernel, ny, nz),
        in_specs=[SMEM] + [VMEM] * (ny * len(chunks)),
        out_specs=[VMEM] * nz,
        out_shape=[jax.ShapeDtypeStruct((q, rank), F32)] * nz,
        compiler_params=params(8),
        name="cut",
    )(where, *[x for c in chunks for x in c])


def join_kernel(nz, *refs):
    where, pieces, outs = refs[0], refs[1:1 + nz], refs[1 + nz:]
    each = nz // len(outs)
    if each == nz:
        for r in range(nz):
            outs[0][where[1] ^ r] = pieces[r][...]
        return
    for t in range(nz):
        for r in range(nz):
            @pl.when((where[1] ^ t) == r)
            def _():
                outs[t // each][t % each] = pieces[r][...]


def join(where, pieces, chunks):
    nz = len(pieces)
    shape = (nz // chunks,) + pieces[0].shape
    return pl.pallas_call(
        functools.partial(join_kernel, nz),
        in_specs=[SMEM] + [VMEM] * nz,
        out_specs=[VMEM] * chunks,
        out_shape=[jax.ShapeDtypeStruct(shape, F32)] * chunks,
        compiler_params=params(8),
        name="join",
    )(where, *pieces)


def pick_kernel(cut, *refs):
    where, olds, out = refs[0], refs[1:-1], refs[-1]
    for c in range(len(olds)):
        @pl.when(lax.div(where[1], cut) == c)
        def _():
            out[...] = olds[c][...]


def pick(where, olds, cut):
    return pl.pallas_call(
        functools.partial(pick_kernel, cut),
        in_specs=[SMEM] + [VMEM] * len(olds),
        out_specs=VMEM,
        out_shape=jax.ShapeDtypeStruct(olds[0].shape, F32),
        compiler_params=params(8),
        name="pick",
    )(where, *olds)


def new_rows(old, terms):
    total = functools.reduce(jnp.add, terms)
    return old + 0.005 * (total - 0.05 * old)


def per_device(n_group, n_sub, users, items, ratings, occupancy):
    strata = ratings.shape[0]
    share, rank = items.shape
    ny = 1
    while ny * ny * 2 <= n_sub:
        ny *= 2
    nz = n_sub // ny
    chunks = max(1, min(CHUNKS, share // 8))
    k = lax.axis_index("sub")
    where = jnp.stack([k & (ny - 1), k >> (ny.bit_length() - 1)]).astype(jnp.int32)

    def over_y(x, r):
        return lax.ppermute(x, "sub", [(i, i ^ r) for i in range(n_sub)])

    def over_z(x, r):
        return lax.ppermute(x, "sub", [(i, i ^ (r * ny)) for i in range(n_sub)])

    def onward(x, r):
        route = []
        for g in range(n_group):
            for i in range(n_sub):
                route.append((g * n_sub + i, (g + 1) % n_group * n_sub + (i ^ (r * ny))))
        return lax.ppermute(x, ("group", "sub"), route)

    q = share // chunks
    owns = join(where, [items] + [over_z(items, r) for r in range(1, nz)], chunks)
    pieces = [[own] + [over_y(own, r) for r in range(1, ny)] for own in owns]

    for s in range(strata):
        last = s == strata - 1
        parts, grads, olds = [], [], []
        for c in range(chunks):
            res = gradients(where, occupancy, users, ratings, pieces[c], s, c, share if last else q)
            parts.append(res[:4])
            olds.append(res[4])
            grads.append([res[5]] + [over_y(res[5 + r], r) for r in range(1, ny)])
        new_users = user_step(users, parts)
        if last:
            old = onward(pick(where, olds, nz // chunks), 0)
            cuts = cut(where, grads)
            rows = new_rows(old, [onward(cuts[r], r) for r in range(nz)])
            return new_users, rows
        for c in range(chunks):
            cuts = cut(where, [grads[c]])
            rows = new_rows(olds[c], [cuts[0]] + [over_z(cuts[r], r) for r in range(1, nz)])
            own = join(where, [onward(rows, r) for r in range(nz)], 1)[0]
            pieces[c] = [own] + [over_y(own, r) for r in range(1, ny)]
        users = new_users


def solution(mesh):
    spec = P(("group", "sub"), None)
    third = P(None, ("group", "sub"), None)
    return jax.shard_map(
        functools.partial(per_device, mesh.shape["group"], mesh.shape["sub"]),
        mesh=mesh,
        in_specs=(spec, spec, third, third),
        out_specs=(spec, spec),
        check_vma=False,
    )
```

```python
import functools

import jax
import jax.numpy as jnp
from jax import lax
from jax.experimental import pallas as pl
from jax.experimental.pallas import tpu as pltpu
from jax.sharding import PartitionSpec as P

TILE = 128
CHUNKS = 2
BLOCK = 512
VMEM = pl.BlockSpec(memory_space=pltpu.VMEM)
SMEM = pl.BlockSpec(memory_space=pltpu.SMEM)
F32 = jnp.float32
BF16 = jnp.bfloat16


def split(x):
    hi = x.astype(BF16)
    return hi, (x - hi.astype(F32)).astype(BF16)


def dot3(a, b, dims):
    (ah, al), (bh, bl) = a, b
    dot = functools.partial(lax.dot_general, dimension_numbers=(dims, ((), ())), preferred_element_type=F32)
    return dot(ah, bh) + (dot(ah, bl) + dot(al, bh))


def params(mib):
    return pltpu.CompilerParams(vmem_limit_bytes=mib * 1024 * 1024)


def grad_kernel(ny, chunk, stratum, *refs):
    where, occ, users, rate = refs[:4]
    pieces = refs[4:4 + ny]
    err_hi, err_lo, v_hi, v_lo, old = refs[4 + ny:9 + ny]
    grads = refs[9 + ny:9 + 2 * ny]
    block, total, vt_hi, vt_lo = refs[9 + 2 * ny:]
    mine = where[0]
    rows, rank = total.shape
    steps, q_in, _ = pieces[0].shape
    for r in range(ny):
        for z in range(steps):
            block[pl.ds((z * ny + (mine ^ r)) * q_in, q_in), :] = pieces[r][z]
    v = block[...]
    v_hi[...], v_lo[...] = split(v)
    vt_hi[...], vt_lo[...] = split(v.T)
    cut, q, _ = grads[0].shape
    old[...] = block[pl.ds((lax.rem(where[1], cut) * ny + mine) * q, q), :]
    for first in range(0, users.shape[0], BLOCK):
        at = slice(first, first + BLOCK)
        u = split(users[at, :])
        pred = dot3(u, (vt_hi[...], vt_lo[...]), ((1,), (0,)))
        err = rate[stratum, at, chunk * rows:(chunk + 1) * rows].astype(F32) - pred
        parts = []
        for a in range(BLOCK // TILE):
            line = []
            for b in range(rows // TILE):
                seen = occ[stratum, first // TILE + a, chunk * rows // TILE + b]
                part = err[a * TILE:(a + 1) * TILE, b * TILE:(b + 1) * TILE]
                line.append(jnp.where(seen == 1, part, 0.0))
            parts.append(jnp.concatenate(line, axis=1))
        err = jnp.concatenate(parts, axis=0)
        err_hi[at, :], err_lo[at, :] = split(err)
        term = dot3(split(err.T), u, ((1,), (0,)))
        if first == 0:
            total[...] = term
        else:
            total[...] += term
    for r in range(ny):
        for z in range(cut):
            grads[r][z] = total[pl.ds((z * ny + (mine ^ r)) * q, q), :]


def gradients(where, occ, users, ratings, pieces, stratum, chunk, q):
    ny = len(pieces)
    steps, q_in, rank = pieces[0].shape
    rows = steps * ny * q_in
    n_users = users.shape[0]
    gshape = (rows // (ny * q), q, rank)
    return pl.pallas_call(
        functools.partial(grad_kernel, ny, chunk, stratum),
        in_specs=[SMEM, SMEM] + [VMEM] * (2 + ny),
        out_specs=[VMEM] * (5 + ny),
        out_shape=[jax.ShapeDtypeStruct((n_users, rows), BF16)] * 2 + [jax.ShapeDtypeStruct((rows, rank), BF16)] * 2
        + [jax.ShapeDtypeStruct((q, rank), F32)] + [jax.ShapeDtypeStruct(gshape, F32)] * ny,
        scratch_shapes=[pltpu.VMEM((rows, rank), F32)] * 2 + [pltpu.VMEM((rank, rows), BF16)] * 2,
        compiler_params=params(24),
        cost_estimate=pl.CostEstimate(flops=12 * n_users * rows * rank, bytes_accessed=4 * n_users * rank, transcendentals=0),
        name="gradients",
    )(where, occ, users, ratings, *pieces)


def step_kernel(n, *refs):
    users, out = refs[0], refs[-1]
    for first in range(0, users.shape[0], BLOCK):
        at = slice(first, first + BLOCK)
        u = users[at, :]
        pull = None
        for i in range(n):
            eh, el, vh, vl = refs[1 + 4 * i:5 + 4 * i]
            part = dot3((eh[at, :], el[at, :]), (vh[...], vl[...]), ((1,), (0,)))
            pull = part if pull is None else pull + part
        out[at, :] = u + 0.02 * (pull - 0.05 * u)


def user_step(users, parts):
    n_users, rank = users.shape
    rows = sum(p[2].shape[0] for p in parts)
    return pl.pallas_call(
        functools.partial(step_kernel, len(parts)),
        in_specs=[VMEM] * (1 + 4 * len(parts)),
        out_specs=VMEM,
        out_shape=jax.ShapeDtypeStruct(users.shape, F32),
        compiler_params=params(24),
        cost_estimate=pl.CostEstimate(flops=6 * n_users * rows * rank, bytes_accessed=8 * n_users * rank, transcendentals=0),
        name="user_step",
    )(users, *[x for p in parts for x in p])


def cut_kernel(ny, nz, *refs):
    where, outs = refs[0], refs[-nz:]
    terms = refs[1:-nz]
    chunks = [terms[i:i + ny] for i in range(0, len(terms), ny)]
    each = nz // len(chunks)
    for t in range(nz):
        parts = [x[t % each] for x in chunks[t // each]]
        total = functools.reduce(jnp.add, parts)
        for r in range(nz):
            @pl.when((where[1] ^ t) == r)
            def _():
                outs[r][...] = total


def cut(where, chunks):
    ny = len(chunks[0])
    each, q, rank = chunks[0][0].shape
    nz = each * len(chunks)
    return pl.pallas_call(
        functools.partial(cut_kernel, ny, nz),
        in_specs=[SMEM] + [VMEM] * (ny * len(chunks)),
        out_specs=[VMEM] * nz,
        out_shape=[jax.ShapeDtypeStruct((q, rank), F32)] * nz,
        compiler_params=params(8),
        name="cut",
    )(where, *[x for c in chunks for x in c])


def join_kernel(nz, *refs):
    where, pieces, outs = refs[0], refs[1:1 + nz], refs[1 + nz:]
    each = nz // len(outs)
    if each == nz:
        for r in range(nz):
            outs[0][where[1] ^ r] = pieces[r][...]
        return
    for t in range(nz):
        for r in range(nz):
            @pl.when((where[1] ^ t) == r)
            def _():
                outs[t // each][t % each] = pieces[r][...]


def join(where, pieces, chunks):
    nz = len(pieces)
    shape = (nz // chunks,) + pieces[0].shape
    return pl.pallas_call(
        functools.partial(join_kernel, nz),
        in_specs=[SMEM] + [VMEM] * nz,
        out_specs=[VMEM] * chunks,
        out_shape=[jax.ShapeDtypeStruct(shape, F32)] * chunks,
        compiler_params=params(8),
        name="join",
    )(where, *pieces)


def pick_kernel(cut, *refs):
    where, olds, out = refs[0], refs[1:-1], refs[-1]
    for c in range(len(olds)):
        @pl.when(lax.div(where[1], cut) == c)
        def _():
            out[...] = olds[c][...]


def pick(where, olds, cut):
    return pl.pallas_call(
        functools.partial(pick_kernel, cut),
        in_specs=[SMEM] + [VMEM] * len(olds),
        out_specs=VMEM,
        out_shape=jax.ShapeDtypeStruct(olds[0].shape, F32),
        compiler_params=params(8),
        name="pick",
    )(where, *olds)


def new_rows(old, terms):
    total = functools.reduce(jnp.add, terms)
    return old + 0.005 * (total - 0.05 * old)


def per_device(n_group, n_sub, users, items, ratings, occupancy):
    strata = ratings.shape[0]
    share, rank = items.shape
    ny = 1
    while ny * ny * 2 <= n_sub:
        ny *= 2
    nz = n_sub // ny
    chunks = max(1, min(CHUNKS, share // 8))
    k = lax.axis_index("sub")
    where = jnp.stack([k & (ny - 1), k >> (ny.bit_length() - 1)]).astype(jnp.int32)

    def over_y(x, r):
        return lax.ppermute(x, "sub", [(i, i ^ r) for i in range(n_sub)])

    def over_z(x, r):
        return lax.ppermute(x, "sub", [(i, i ^ (r * ny)) for i in range(n_sub)])

    def onward(x, r):
        route = []
        for g in range(n_group):
            for i in range(n_sub):
                route.append((g * n_sub + i, (g + 1) % n_group * n_sub + (i ^ r)))
        return lax.ppermute(x, ("group", "sub"), route)

    wide = nz * share // chunks
    owns = join(where, [items] + [over_z(items, r) for r in range(1, nz)], chunks)
    pieces = [[own] + [over_y(own, r) for r in range(1, ny)] for own in owns]

    for s in range(strata):
        last = s == strata - 1
        parts, grads, olds = [], [], []
        for c in range(chunks):
            res = gradients(where, occupancy, users, ratings, pieces[c], s, c, share if last else wide)
            parts.append(res[:4])
            olds.append(res[4])
            grads.append([res[5]] + [over_y(res[5 + r], r) for r in range(1, ny)])
        new_users = user_step(users, parts)
        if last:
            old = onward(pick(where, olds, nz // chunks), 0)
            cuts = cut(where, grads)
            rows = new_rows(old, [onward(cuts[r], r * ny) for r in range(nz)])
            return new_users, rows
        for c in range(chunks):
            total = functools.reduce(jnp.add, grads[c])
            for bit in range(1, nz.bit_length()):
                total = total + over_z(total, 1 << (bit - 1))
            rows = new_rows(olds[c].reshape(total.shape), [total])
            pieces[c] = [onward(rows, r) for r in range(ny)]
        users = new_users


def solution(mesh):
    spec = P(("group", "sub"), None)
    third = P(None, ("group", "sub"), None)
    return jax.shard_map(
        functools.partial(per_device, mesh.shape["group"], mesh.shape["sub"]),
        mesh=mesh,
        in_specs=(spec, spec, third, third),
        out_specs=(spec, spec),
        check_vma=False,
    )
```

```python
import functools

import jax
import jax.numpy as jnp
from jax import lax
from jax.experimental import pallas as pl
from jax.experimental.pallas import tpu as pltpu
from jax.sharding import PartitionSpec as P

TILE = 128
CHUNKS = 2
BLOCK = 512
VMEM = pl.BlockSpec(memory_space=pltpu.VMEM)
SMEM = pl.BlockSpec(memory_space=pltpu.SMEM)
F32 = jnp.float32
BF16 = jnp.bfloat16


def split(x):
    hi = x.astype(BF16)
    return hi, (x - hi.astype(F32)).astype(BF16)


def dot3(a, b, dims):
    (ah, al), (bh, bl) = a, b
    dot = functools.partial(lax.dot_general, dimension_numbers=(dims, ((), ())), preferred_element_type=F32)
    return dot(ah, bh) + (dot(ah, bl) + dot(al, bh))


def place(ny):
    k = lax.axis_index("sub")
    return k & (ny - 1), lax.shift_right_logical(k, ny.bit_length() - 1)


def params(mib):
    return pltpu.CompilerParams(vmem_limit_bytes=mib * 1024 * 1024)


def grad_kernel(ny, chunk, stratum, *refs):
    occ, users, rate = refs[:3]
    where = place(ny)
    pieces = refs[3:3 + ny]
    err_hi, err_lo, v_hi, v_lo, old = refs[3 + ny:8 + ny]
    grads = refs[8 + ny:8 + 2 * ny]
    block, total, vt_hi, vt_lo = refs[8 + 2 * ny:]
    mine = where[0]
    rows, rank = total.shape
    steps, q_in, _ = pieces[0].shape
    for r in range(ny):
        for z in range(steps):
            block[pl.ds((z * ny + (mine ^ r)) * q_in, q_in), :] = pieces[r][z]
    v = block[...]
    v_hi[...], v_lo[...] = split(v)
    vt_hi[...], vt_lo[...] = split(v.T)
    cut, q, _ = grads[0].shape
    old[...] = block[pl.ds((lax.rem(where[1], cut) * ny + mine) * q, q), :]
    for first in range(0, users.shape[0], BLOCK):
        at = slice(first, first + BLOCK)
        u = split(users[at, :])
        pred = dot3(u, (vt_hi[...], vt_lo[...]), ((1,), (0,)))
        err = rate[stratum, at, chunk * rows:(chunk + 1) * rows].astype(F32) - pred
        parts = []
        for a in range(BLOCK // TILE):
            line = []
            for b in range(rows // TILE):
                seen = occ[stratum, chunk * rows // TILE + b, first // TILE + a]
                part = err[a * TILE:(a + 1) * TILE, b * TILE:(b + 1) * TILE]
                line.append(jnp.where(seen == 1, part, 0.0))
            parts.append(jnp.concatenate(line, axis=1))
        err = jnp.concatenate(parts, axis=0)
        err_hi[at, :], err_lo[at, :] = split(err)
        term = dot3(split(err.T), u, ((1,), (0,)))
        if first == 0:
            total[...] = term
        else:
            total[...] += term
    for r in range(ny):
        for z in range(cut):
            grads[r][z] = total[pl.ds((z * ny + (mine ^ r)) * q, q), :]


def gradients(occ, users, ratings, pieces, stratum, chunk, q):
    ny = len(pieces)
    steps, q_in, rank = pieces[0].shape
    rows = steps * ny * q_in
    n_users = users.shape[0]
    gshape = (rows // (ny * q), q, rank)
    return pl.pallas_call(
        functools.partial(grad_kernel, ny, chunk, stratum),
        in_specs=[SMEM] + [VMEM] * (2 + ny),
        out_specs=[VMEM] * (5 + ny),
        out_shape=[jax.ShapeDtypeStruct((n_users, rows), BF16)] * 2 + [jax.ShapeDtypeStruct((rows, rank), BF16)] * 2
        + [jax.ShapeDtypeStruct((q, rank), F32)] + [jax.ShapeDtypeStruct(gshape, F32)] * ny,
        scratch_shapes=[pltpu.VMEM((rows, rank), F32)] * 2 + [pltpu.VMEM((rank, rows), BF16)] * 2,
        compiler_params=params(24),
        cost_estimate=pl.CostEstimate(flops=12 * n_users * rows * rank, bytes_accessed=4 * n_users * rank, transcendentals=0),
        name="gradients",
    )(occ, users, ratings, *pieces)


def step_kernel(n, *refs):
    users, out = refs[0], refs[-1]
    for first in range(0, users.shape[0], BLOCK):
        at = slice(first, first + BLOCK)
        u = users[at, :]
        pull = None
        for i in range(n):
            eh, el, vh, vl = refs[1 + 4 * i:5 + 4 * i]
            part = dot3((eh[at, :], el[at, :]), (vh[...], vl[...]), ((1,), (0,)))
            pull = part if pull is None else pull + part
        out[at, :] = u + 0.02 * (pull - 0.05 * u)


def user_step(users, parts):
    n_users, rank = users.shape
    rows = sum(p[2].shape[0] for p in parts)
    return pl.pallas_call(
        functools.partial(step_kernel, len(parts)),
        in_specs=[VMEM] * (1 + 4 * len(parts)),
        out_specs=VMEM,
        out_shape=jax.ShapeDtypeStruct(users.shape, F32),
        compiler_params=params(24),
        cost_estimate=pl.CostEstimate(flops=6 * n_users * rows * rank, bytes_accessed=8 * n_users * rank, transcendentals=0),
        name="user_step",
    )(users, *[x for p in parts for x in p])


def cut_kernel(ny, nz, *refs):
    where, outs = place(ny), refs[-nz:]
    terms = refs[:-nz]
    chunks = [terms[i:i + ny] for i in range(0, len(terms), ny)]
    each = nz // len(chunks)
    for t in range(nz):
        parts = [x[t % each] for x in chunks[t // each]]
        total = functools.reduce(jnp.add, parts)
        for r in range(nz):
            @pl.when((where[1] ^ t) == r)
            def _():
                outs[r][...] = total


def cut(chunks):
    ny = len(chunks[0])
    each, q, rank = chunks[0][0].shape
    nz = each * len(chunks)
    return pl.pallas_call(
        functools.partial(cut_kernel, ny, nz),
        in_specs=[VMEM] * (ny * len(chunks)),
        out_specs=[VMEM] * nz,
        out_shape=[jax.ShapeDtypeStruct((q, rank), F32)] * nz,
        compiler_params=params(8),
        name="cut",
    )(*[x for c in chunks for x in c])


def join_kernel(ny, nz, *refs):
    where, pieces, outs = place(ny), refs[:nz], refs[nz:]
    each = nz // len(outs)
    if each == nz:
        for r in range(nz):
            outs[0][where[1] ^ r] = pieces[r][...]
        return
    for t in range(nz):
        for r in range(nz):
            @pl.when((where[1] ^ t) == r)
            def _():
                outs[t // each][t % each] = pieces[r][...]


def join(ny, pieces, chunks):
    nz = len(pieces)
    shape = (nz // chunks,) + pieces[0].shape
    return pl.pallas_call(
        functools.partial(join_kernel, ny, nz),
        in_specs=[VMEM] * nz,
        out_specs=[VMEM] * chunks,
        out_shape=[jax.ShapeDtypeStruct(shape, F32)] * chunks,
        compiler_params=params(8),
        name="join",
    )(*pieces)


def pick_kernel(ny, cut, *refs):
    where, olds, out = place(ny), refs[:-1], refs[-1]
    for c in range(len(olds)):
        @pl.when(lax.div(where[1], cut) == c)
        def _():
            out[...] = olds[c][...]


def pick(ny, olds, cut):
    return pl.pallas_call(
        functools.partial(pick_kernel, ny, cut),
        in_specs=[VMEM] * len(olds),
        out_specs=VMEM,
        out_shape=jax.ShapeDtypeStruct(olds[0].shape, F32),
        compiler_params=params(8),
        name="pick",
    )(*olds)


def new_rows(old, terms):
    total = functools.reduce(jnp.add, terms)
    return old + 0.005 * (total - 0.05 * old)


def per_device(n_group, n_sub, users, items, ratings, occupancy):
    strata = ratings.shape[0]
    share, rank = items.shape
    ny = 1
    while ny * ny * 2 <= n_sub:
        ny *= 2
    nz = n_sub // ny
    chunks = max(1, min(CHUNKS, share // 8))

    def over_y(x, r):
        return lax.ppermute(x, "sub", [(i, i ^ r) for i in range(n_sub)])

    def over_z(x, r):
        return lax.ppermute(x, "sub", [(i, i ^ (r * ny)) for i in range(n_sub)])

    def onward(x, r):
        route = []
        for g in range(n_group):
            for i in range(n_sub):
                route.append((g * n_sub + i, (g + 1) % n_group * n_sub + (i ^ r)))
        return lax.ppermute(x, ("group", "sub"), route)

    occupancy = occupancy.transpose(0, 2, 1)

    wide = nz * share // chunks
    owns = join(ny, [items] + [over_z(items, r) for r in range(1, nz)], chunks)
    pieces = [[own] + [over_y(own, r) for r in range(1, ny)] for own in owns]

    for s in range(strata):
        last = s == strata - 1
        parts, grads, olds = [], [], []
        for c in range(chunks):
            res = gradients(occupancy, users, ratings, pieces[c], s, c, share if last else wide)
            parts.append(res[:4])
            olds.append(res[4])
            grads.append([res[5]] + [over_y(res[5 + r], r) for r in range(1, ny)])
        new_users = user_step(users, parts)
        if last:
            old = onward(pick(ny, olds, nz // chunks), 0)
            cuts = cut(grads)
            rows = new_rows(old, [onward(cuts[r], r * ny) for r in range(nz)])
            return new_users, rows
        for c in range(chunks):
            total = functools.reduce(jnp.add, grads[c])
            for bit in range(1, nz.bit_length()):
                total = total + over_z(total, 1 << (bit - 1))
            own = onward(new_rows(olds[c].reshape(total.shape), [total]), 0)
            pieces[c] = [own] + [over_y(own, r) for r in range(1, ny)]
        users = new_users


def solution(mesh):
    spec = P(("group", "sub"), None)
    third = P(None, ("group", "sub"), None)
    return jax.shard_map(
        functools.partial(per_device, mesh.shape["group"], mesh.shape["sub"]),
        mesh=mesh,
        in_specs=(spec, spec, third, third),
        out_specs=(spec, spec),
        check_vma=False,
    )
```

```python
import functools

import jax
import jax.numpy as jnp
from jax import lax
from jax.experimental import pallas as pl
from jax.experimental.pallas import tpu as pltpu
from jax.sharding import PartitionSpec as P

TILE = 128
BLOCK = 512
VMEM = pl.BlockSpec(memory_space=pltpu.VMEM)
SMEM = pl.BlockSpec(memory_space=pltpu.SMEM)
F32 = jnp.float32
BF16 = jnp.bfloat16


def split(x):
    hi = x.astype(BF16)
    return hi, (x - hi.astype(F32)).astype(BF16)


def dot3(a, b, dims):
    (ah, al), (bh, bl) = a, b
    dot = functools.partial(lax.dot_general, dimension_numbers=(dims, ((), ())), preferred_element_type=F32)
    return dot(ah, bh) + (dot(ah, bl) + dot(al, bh))


def params(mib):
    return pltpu.CompilerParams(vmem_limit_bytes=mib * 1024 * 1024)


def load_kernel(users, ratings, users_out, ratings_out, sems):
    copies = [pltpu.make_async_copy(users, users_out, sems.at[0]), pltpu.make_async_copy(ratings, ratings_out, sems.at[1])]
    for copy in copies:
        copy.start()
    for copy in copies:
        copy.wait()


def load(users, ratings):
    return pl.pallas_call(
        load_kernel,
        in_specs=[pl.BlockSpec(memory_space=pltpu.HBM)] * 2,
        out_specs=[VMEM] * 2,
        out_shape=[jax.ShapeDtypeStruct(users.shape, F32), jax.ShapeDtypeStruct(ratings.shape, BF16)],
        scratch_shapes=[pltpu.SemaphoreType.DMA((2,))],
        compiler_params=params(12),
        cost_estimate=pl.CostEstimate(flops=0, bytes_accessed=2 * (users.size * 4 + ratings.size * 2), transcendentals=0),
        name="load",
    )(users, ratings)


def grad_kernel(ny, place, stratum, *refs):
    occ, users, rate = refs[:3]
    pieces = refs[3:3 + ny]
    err_hi, err_lo, v_hi, v_lo = refs[3 + ny:7 + ny]
    grads = refs[7 + ny:7 + 2 * ny]
    block, total, vt_hi, vt_lo = refs[7 + 2 * ny:]
    k = lax.axis_index("sub")
    mine = k & (ny - 1)
    chunk = (lax.shift_right_logical(k, ny.bit_length() - 1) + (place + stratum)) & 1
    rows, rank = total.shape
    q = pieces[0].shape[0]
    for r in range(ny):
        block[pl.ds((mine ^ r) * q, q), :] = pieces[r][...]
    v = block[...]
    v_hi[...], v_lo[...] = split(v)
    vt_hi[...], vt_lo[...] = split(v.T)
    columns = pl.ds(pl.multiple_of(chunk * rows, TILE), rows)
    for first in range(0, users.shape[0], BLOCK):
        at = slice(first, first + BLOCK)
        u = split(users[at, :])
        pred = dot3(u, (vt_hi[...], vt_lo[...]), ((1,), (0,)))
        err = rate[stratum, at, columns].astype(F32) - pred
        parts = []
        for a in range(BLOCK // TILE):
            line = []
            for b in range(rows // TILE):
                seen = occ[stratum, chunk * (rows // TILE) + b, first // TILE + a]
                part = err[a * TILE:(a + 1) * TILE, b * TILE:(b + 1) * TILE]
                line.append(jnp.where(seen == 1, part, 0.0))
            parts.append(jnp.concatenate(line, axis=1))
        err = jnp.concatenate(parts, axis=0)
        err_hi[at, :], err_lo[at, :] = split(err)
        term = dot3(split(err.T), u, ((1,), (0,)))
        if first == 0:
            total[...] = term
        else:
            total[...] += term
    for r in range(ny):
        grads[r][...] = total[pl.ds((mine ^ r) * q, q), :]


def gradients(occ, users, ratings, pieces, place, stratum):
    ny = len(pieces)
    q, rank = pieces[0].shape
    rows = ny * q
    n_users = users.shape[0]
    return pl.pallas_call(
        functools.partial(grad_kernel, ny, place, stratum),
        in_specs=[SMEM] + [VMEM] * (2 + ny),
        out_specs=[VMEM] * (4 + ny),
        out_shape=[jax.ShapeDtypeStruct((n_users, rows), BF16)] * 2 + [jax.ShapeDtypeStruct((rows, rank), BF16)] * 2
        + [jax.ShapeDtypeStruct((q, rank), F32)] * ny,
        scratch_shapes=[pltpu.VMEM((rows, rank), F32)] * 2 + [pltpu.VMEM((rank, rows), BF16)] * 2,
        compiler_params=params(24),
        cost_estimate=pl.CostEstimate(flops=12 * n_users * rows * rank, bytes_accessed=4 * n_users * rank, transcendentals=0),
        name="gradients",
    )(occ, users, ratings, *pieces)


def step_kernel(n, *refs):
    users, out = refs[0], refs[-1]
    for first in range(0, users.shape[0], BLOCK):
        at = slice(first, first + BLOCK)
        u = users[at, :]
        pull = None
        for i in range(n):
            eh, el, vh, vl = refs[1 + 4 * i:5 + 4 * i]
            part = dot3((eh[at, :], el[at, :]), (vh[...], vl[...]), ((1,), (0,)))
            pull = part if pull is None else pull + part
        out[at, :] = u + 0.02 * (pull - 0.05 * u)


def user_step(users, parts):
    n_users, rank = users.shape
    rows = sum(p[2].shape[0] for p in parts)
    return pl.pallas_call(
        functools.partial(step_kernel, len(parts)),
        in_specs=[VMEM] * (1 + 4 * len(parts)),
        out_specs=VMEM,
        out_shape=jax.ShapeDtypeStruct(users.shape, F32),
        compiler_params=params(24),
        cost_estimate=pl.CostEstimate(flops=6 * n_users * rows * rank, bytes_accessed=8 * n_users * rank, transcendentals=0),
        name="user_step",
    )(users, *[x for p in parts for x in p])


def per_device(n_group, n_sub, users, items, ratings, occupancy):
    strata = ratings.shape[0]
    ny = n_sub // 2
    occupancy = occupancy.transpose(0, 2, 1)

    def over_y(x, r):
        return lax.ppermute(x, "sub", [(i, i ^ r) for i in range(n_sub)])

    def onward(x, r):
        route = []
        for g in range(n_group):
            for i in range(n_sub):
                route.append((g * n_sub + i, (g + 1) % n_group * n_sub + (i ^ r)))
        return lax.ppermute(x, ("group", "sub"), route)

    def gathered(own):
        return [own] + [over_y(own, r) for r in range(1, ny)]

    def summed(terms):
        return functools.reduce(jnp.add, [terms[0]] + [over_y(terms[r], r) for r in range(1, ny)])

    first = gathered(items)
    second = gathered(over_y(items, ny))
    users, ratings = load(users, ratings)
    for s in range(strata):
        one = gradients(occupancy, users, ratings, first, 0, s)
        term = summed(one[4:])
        base = first[0] + 0.005 * (term - 0.05 * first[0])
        two = gradients(occupancy, users, ratings, second, 1, s)
        users = user_step(users, [one[:4], two[:4]])
        term = summed(two[4:])
        if s < strata - 1:
            near = onward(base, ny) + 0.005 * onward(term, 0)
            far = onward(base, 0) + 0.005 * onward(term, ny)
            first, second = gathered(near), gathered(far)
        elif strata % 2 == 0:
            return users, onward(base, ny) + 0.005 * onward(term, 0)
        else:
            return users, onward(base, 0) + 0.005 * onward(term, ny)


def solution(mesh):
    spec = P(("group", "sub"), None)
    third = P(None, ("group", "sub"), None)
    return jax.shard_map(
        functools.partial(per_device, mesh.shape["group"], mesh.shape["sub"]),
        mesh=mesh,
        in_specs=(spec, spec, third, third),
        out_specs=(spec, spec),
        check_vma=False,
    )
```

```python
import functools

import jax
import jax.numpy as jnp
from jax import lax
from jax.experimental import pallas as pl
from jax.experimental.pallas import tpu as pltpu
from jax.sharding import PartitionSpec as P

TILE = 128
BLOCK = 512
VMEM = pl.BlockSpec(memory_space=pltpu.VMEM)
SMEM = pl.BlockSpec(memory_space=pltpu.SMEM)
F32 = jnp.float32
BF16 = jnp.bfloat16


def split(x):
    hi = x.astype(BF16)
    return hi, (x - hi.astype(F32)).astype(BF16)


def dot3(a, b, dims):
    (ah, al), (bh, bl) = a, b
    dot = functools.partial(lax.dot_general, dimension_numbers=(dims, ((), ())), preferred_element_type=F32)
    return dot(ah, bh) + (dot(ah, bl) + dot(al, bh))


def params(mib):
    return pltpu.CompilerParams(vmem_limit_bytes=mib * 1024 * 1024)


def load_kernel(users, ratings, users_out, turned, held, sems):
    strata = ratings.shape[0]
    copies = [pltpu.make_async_copy(ratings.at[s], held.at[s], sems.at[s]) for s in range(strata)]
    copies.append(pltpu.make_async_copy(users, users_out, sems.at[strata]))
    for copy in copies:
        copy.start()
    for s in range(strata):
        copies[s].wait()
        turned[s] = held[s].T
    copies[strata].wait()


def load(users, ratings):
    strata, n_users, items = ratings.shape
    return pl.pallas_call(
        load_kernel,
        in_specs=[pl.BlockSpec(memory_space=pl.ANY)] * 2,
        out_specs=[VMEM] * 2,
        out_shape=[jax.ShapeDtypeStruct(users.shape, F32), jax.ShapeDtypeStruct((strata, items, n_users), BF16)],
        scratch_shapes=[pltpu.VMEM(ratings.shape, BF16), pltpu.SemaphoreType.DMA((strata + 1,))],
        compiler_params=params(44),
        cost_estimate=pl.CostEstimate(flops=0, bytes_accessed=2 * (users.size * 4 + ratings.size * 2), transcendentals=0),
        name="load",
    )(users, ratings)


def grad_kernel(ny, place, stratum, *refs):
    occ, users, rate = refs[:3]
    pieces = refs[3:3 + ny]
    err_hi, err_lo, v_hi, v_lo = refs[3 + ny:7 + ny]
    grads = refs[7 + ny:7 + 2 * ny]
    block, total = refs[7 + 2 * ny:]
    k = lax.axis_index("sub")
    mine = k & (ny - 1)
    chunk = (lax.shift_right_logical(k, ny.bit_length() - 1) + (place + stratum)) & 1
    rows, rank = total.shape
    q = pieces[0].shape[0]
    for r in range(ny):
        block[pl.ds((mine ^ r) * q, q), :] = pieces[r][...]
    v_hi[...], v_lo[...] = split(block[...])
    u = split(users[...])
    pred = dot3((v_hi[...], v_lo[...]), u, ((1,), (1,)))
    at = pl.ds(pl.multiple_of(chunk * rows, TILE), rows)
    err = rate[stratum, at, :].astype(F32) - pred
    parts = []
    for b in range(rows // TILE):
        line = []
        for a in range(err.shape[1] // TILE):
            seen = occ[stratum, chunk * (rows // TILE) + b, a]
            part = err[b * TILE:(b + 1) * TILE, a * TILE:(a + 1) * TILE]
            line.append(jnp.where(seen == 1, part, 0.0))
        parts.append(jnp.concatenate(line, axis=1))
    e = split(jnp.concatenate(parts, axis=0))
    err_hi[...], err_lo[...] = e
    total[...] = dot3(e, u, ((1,), (0,)))
    for r in range(ny):
        grads[r][...] = total[pl.ds((mine ^ r) * q, q), :]


def gradients(occ, users, ratings, pieces, place, stratum):
    ny = len(pieces)
    q, rank = pieces[0].shape
    rows = ny * q
    n_users = users.shape[0]
    return pl.pallas_call(
        functools.partial(grad_kernel, ny, place, stratum),
        in_specs=[SMEM] + [VMEM] * (2 + ny),
        out_specs=[VMEM] * (4 + ny),
        out_shape=[jax.ShapeDtypeStruct((rows, n_users), BF16)] * 2 + [jax.ShapeDtypeStruct((rows, rank), BF16)] * 2
        + [jax.ShapeDtypeStruct((q, rank), F32)] * ny,
        scratch_shapes=[pltpu.VMEM((rows, rank), F32)] * 2,
        compiler_params=params(24),
        cost_estimate=pl.CostEstimate(flops=12 * n_users * rows * rank, bytes_accessed=4 * n_users * rank, transcendentals=0),
        name="gradients",
    )(occ, users, ratings, *pieces)


def step_kernel(n, *refs):
    users, out = refs[0], refs[-1]
    for first in range(0, users.shape[0], BLOCK):
        at = slice(first, first + BLOCK)
        u = users[at, :]
        pull = None
        for i in range(n):
            eh, el, vh, vl = refs[1 + 4 * i:5 + 4 * i]
            part = dot3((eh[:, at], el[:, at]), (vh[...], vl[...]), ((0,), (0,)))
            pull = part if pull is None else pull + part
        out[at, :] = u + 0.02 * (pull - 0.05 * u)


def user_step(users, parts):
    n_users, rank = users.shape
    rows = sum(p[2].shape[0] for p in parts)
    return pl.pallas_call(
        functools.partial(step_kernel, len(parts)),
        in_specs=[VMEM] * (1 + 4 * len(parts)),
        out_specs=VMEM,
        out_shape=jax.ShapeDtypeStruct(users.shape, F32),
        compiler_params=params(24),
        cost_estimate=pl.CostEstimate(flops=6 * n_users * rows * rank, bytes_accessed=8 * n_users * rank, transcendentals=0),
        name="user_step",
    )(users, *[x for p in parts for x in p])


def per_device(n_group, n_sub, users, items, ratings, occupancy):
    strata = ratings.shape[0]
    ny = n_sub // 2
    occupancy = occupancy.transpose(0, 2, 1)

    def over_y(x, r):
        return lax.ppermute(x, "sub", [(i, i ^ r) for i in range(n_sub)])

    def onward(x, r):
        route = []
        for g in range(n_group):
            for i in range(n_sub):
                route.append((g * n_sub + i, (g + 1) % n_group * n_sub + (i ^ r)))
        return lax.ppermute(x, ("group", "sub"), route)

    def gathered(own):
        return [own] + [over_y(own, r) for r in range(1, ny)]

    def arrived(terms):
        return [terms[0]] + [over_y(terms[r], r) for r in range(1, ny)]

    first = gathered(items)
    second = gathered(over_y(items, ny))
    users, ratings = load(users, ratings)
    for s in range(strata):
        last = s == strata - 1
        one = gradients(occupancy, users, ratings, first, 0, s)
        second, _ = lax.optimization_barrier((second, one[4]))
        two = gradients(occupancy, users, ratings, second, 1, s)
        term = arrived(one[4:])
        users, term[1] = lax.optimization_barrier((users, term[1]))
        users = user_step(users, [one[:4], two[:4]])
        term, users = lax.optimization_barrier((functools.reduce(jnp.add, term), users))
        base = first[0] + 0.005 * (term - 0.05 * first[0])
        term = functools.reduce(jnp.add, arrived(two[4:]))
        flip = strata % 2 if last else 0
        near = onward(base, 0 if flip else ny) + 0.005 * onward(term, ny if flip else 0)
        if last:
            return users, near
        far = onward(base, 0) + 0.005 * onward(term, ny)
        first, second = gathered(near), gathered(far)


def solution(mesh):
    spec = P(("group", "sub"), None)
    third = P(None, ("group", "sub"), None)
    return jax.shard_map(
        functools.partial(per_device, mesh.shape["group"], mesh.shape["sub"]),
        mesh=mesh,
        in_specs=(spec, spec, third, third),
        out_specs=(spec, spec),
        check_vma=False,
    )
```

```python
import functools

import jax
import jax.numpy as jnp
from jax import lax
from jax.experimental import pallas as pl
from jax.experimental.pallas import tpu as pltpu
from jax.sharding import PartitionSpec as P

TILE = 128
BLOCK = 512
VMEM = pl.BlockSpec(memory_space=pltpu.VMEM)
SMEM = pl.BlockSpec(memory_space=pltpu.SMEM)
F32 = jnp.float32
BF16 = jnp.bfloat16


def split(x):
    hi = x.astype(BF16)
    return hi, (x - hi.astype(F32)).astype(BF16)


def dot3(a, b, dims):
    (ah, al), (bh, bl) = a, b
    dot = functools.partial(lax.dot_general, dimension_numbers=(dims, ((), ())), preferred_element_type=F32)
    return dot(ah, bh) + (dot(ah, bl) + dot(al, bh))


def params(mib):
    return pltpu.CompilerParams(vmem_limit_bytes=mib * 1024 * 1024)


def load_kernel(users, ratings, users_out, turned, held, sems):
    strata = ratings.shape[0]
    copies = [pltpu.make_async_copy(ratings.at[s], held.at[s], sems.at[s]) for s in range(strata)]
    copies.append(pltpu.make_async_copy(users, users_out, sems.at[strata]))
    for copy in copies:
        copy.start()
    for s in range(strata):
        copies[s].wait()
        turned[s] = held[s].T
    copies[strata].wait()


def load(users, ratings):
    strata, n_users, items = ratings.shape
    return pl.pallas_call(
        load_kernel,
        in_specs=[pl.BlockSpec(memory_space=pl.ANY)] * 2,
        out_specs=[VMEM] * 2,
        out_shape=[jax.ShapeDtypeStruct(users.shape, F32), jax.ShapeDtypeStruct((strata, items, n_users), BF16)],
        scratch_shapes=[pltpu.VMEM(ratings.shape, BF16), pltpu.SemaphoreType.DMA((strata + 1,))],
        compiler_params=params(44),
        cost_estimate=pl.CostEstimate(flops=0, bytes_accessed=2 * (users.size * 4 + ratings.size * 2), transcendentals=0),
        name="load",
    )(users, ratings)


def grad_kernel(ny, place, stratum, *refs):
    occ, users, rate = refs[:3]
    pieces = refs[3:3 + ny]
    err_hi, err_lo, v_hi, v_lo = refs[3 + ny:7 + ny]
    grads = refs[7 + ny:7 + 2 * ny]
    block, total = refs[7 + 2 * ny:]
    k = lax.axis_index("sub")
    mine = k & (ny - 1)
    chunk = (lax.shift_right_logical(k, ny.bit_length() - 1) + (place + stratum)) & 1
    rows, rank = total.shape
    q = pieces[0].shape[0]
    for r in range(ny):
        block[pl.ds((mine ^ r) * q, q), :] = pieces[r][...]
    v_hi[...], v_lo[...] = split(block[...])
    u = split(users[...])
    pred = dot3((v_hi[...], v_lo[...]), u, ((1,), (1,)))
    at = pl.ds(pl.multiple_of(chunk * rows, TILE), rows)
    err = rate[stratum, at, :].astype(F32) - pred
    parts = []
    for b in range(rows // TILE):
        line = []
        for a in range(err.shape[1] // TILE):
            seen = occ[stratum, chunk * (rows // TILE) + b, a]
            part = err[b * TILE:(b + 1) * TILE, a * TILE:(a + 1) * TILE]
            line.append(jnp.where(seen == 1, part, 0.0))
        parts.append(jnp.concatenate(line, axis=1))
    e = split(jnp.concatenate(parts, axis=0))
    err_hi[...], err_lo[...] = e
    total[...] = dot3(e, u, ((1,), (0,)))
    for r in range(ny):
        grads[r][...] = total[pl.ds((mine ^ r) * q, q), :]


def gradients(occ, users, ratings, pieces, place, stratum):
    ny = len(pieces)
    q, rank = pieces[0].shape
    rows = ny * q
    n_users = users.shape[0]
    return pl.pallas_call(
        functools.partial(grad_kernel, ny, place, stratum),
        in_specs=[SMEM] + [VMEM] * (2 + ny),
        out_specs=[VMEM] * (4 + ny),
        out_shape=[jax.ShapeDtypeStruct((rows, n_users), BF16)] * 2 + [jax.ShapeDtypeStruct((rows, rank), BF16)] * 2
        + [jax.ShapeDtypeStruct((q, rank), F32)] * ny,
        scratch_shapes=[pltpu.VMEM((rows, rank), F32)] * 2,
        compiler_params=params(24),
        cost_estimate=pl.CostEstimate(flops=12 * n_users * rows * rank, bytes_accessed=4 * n_users * rank, transcendentals=0),
        name="gradients",
    )(occ, users, ratings, *pieces)


def step_kernel(n, *refs):
    users, out = refs[0], refs[-1]
    for first in range(0, users.shape[0], BLOCK):
        at = slice(first, first + BLOCK)
        u = users[at, :]
        pull = None
        for i in range(n):
            eh, el, vh, vl = refs[1 + 4 * i:5 + 4 * i]
            part = dot3((eh[:, at], el[:, at]), (vh[...], vl[...]), ((0,), (0,)))
            pull = part if pull is None else pull + part
        out[at, :] = u + 0.02 * (pull - 0.05 * u)


def user_step(users, parts):
    n_users, rank = users.shape
    rows = sum(p[2].shape[0] for p in parts)
    return pl.pallas_call(
        functools.partial(step_kernel, len(parts)),
        in_specs=[VMEM] * (1 + 4 * len(parts)),
        out_specs=VMEM,
        out_shape=jax.ShapeDtypeStruct(users.shape, F32),
        compiler_params=params(24),
        cost_estimate=pl.CostEstimate(flops=6 * n_users * rows * rank, bytes_accessed=8 * n_users * rank, transcendentals=0),
        name="user_step",
    )(users, *[x for p in parts for x in p])


def per_device(n_group, n_sub, users, items, ratings, occupancy):
    strata = ratings.shape[0]
    ny = n_sub // 2
    occupancy = occupancy.transpose(0, 2, 1)

    def over_y(x, r):
        return lax.ppermute(x, "sub", [(i, i ^ r) for i in range(n_sub)])

    def onward(x, r):
        route = []
        for g in range(n_group):
            for i in range(n_sub):
                route.append((g * n_sub + i, (g + 1) % n_group * n_sub + (i ^ r)))
        return lax.ppermute(x, ("group", "sub"), route)

    def gathered(own):
        return [own] + [over_y(own, r) for r in range(1, ny)]

    def arrived(terms):
        return [terms[0]] + [over_y(terms[r], r) for r in range(1, ny)]

    first = gathered(items)
    second = gathered(over_y(items, ny))
    users, ratings = load(users, ratings)
    for s in range(strata):
        last = s == strata - 1
        one = gradients(occupancy, users, ratings, first, 0, s)
        two = gradients(occupancy, users, ratings, second, 1, s)
        base = functools.reduce(jnp.add, arrived(one[4:]))
        base = first[0] + 0.005 * (base - 0.05 * first[0])
        term = functools.reduce(jnp.add, arrived(two[4:]))
        flip = strata % 2 if last else 0
        near = onward(base, 0 if flip else ny) + 0.005 * onward(term, ny if flip else 0)
        if last:
            return user_step(users, [one[:4], two[:4]]), near
        far = onward(base, 0) + 0.005 * onward(term, ny)
        users, base = lax.optimization_barrier((users, base))
        users = user_step(users, [one[:4], two[:4]])
        first, second = gathered(near), gathered(far)


def solution(mesh):
    spec = P(("group", "sub"), None)
    third = P(None, ("group", "sub"), None)
    return jax.shard_map(
        functools.partial(per_device, mesh.shape["group"], mesh.shape["sub"]),
        mesh=mesh,
        in_specs=(spec, spec, third, third),
        out_specs=(spec, spec),
        check_vma=False,
    )
```

```python
import functools

import jax
import jax.numpy as jnp
from jax import lax
from jax.experimental import pallas as pl
from jax.experimental.pallas import tpu as pltpu
from jax.sharding import PartitionSpec as P

TILE = 128
BLOCK = 512
VMEM = pl.BlockSpec(memory_space=pltpu.VMEM)
SMEM = pl.BlockSpec(memory_space=pltpu.SMEM)
F32 = jnp.float32
BF16 = jnp.bfloat16


def split(x):
    hi = x.astype(BF16)
    return hi, (x - hi.astype(F32)).astype(BF16)


def dot3(a, b, dims):
    (ah, al), (bh, bl) = a, b
    dot = functools.partial(lax.dot_general, dimension_numbers=(dims, ((), ())), preferred_element_type=F32)
    return dot(ah, bh) + (dot(ah, bl) + dot(al, bh))


def params(mib):
    return pltpu.CompilerParams(vmem_limit_bytes=mib * 1024 * 1024)


def load_kernel(users, ratings, users_out, turned, held, sems):
    strata = ratings.shape[0]
    copies = [pltpu.make_async_copy(ratings.at[s], held.at[s], sems.at[s]) for s in range(strata)]
    copies.append(pltpu.make_async_copy(users, users_out, sems.at[strata]))
    for copy in copies:
        copy.start()
    for s in range(strata):
        copies[s].wait()
        turned[s] = held[s].T
    copies[strata].wait()


def load(users, ratings):
    strata, n_users, items = ratings.shape
    return pl.pallas_call(
        load_kernel,
        in_specs=[pl.BlockSpec(memory_space=pl.ANY)] * 2,
        out_specs=[VMEM] * 2,
        out_shape=[jax.ShapeDtypeStruct(users.shape, F32), jax.ShapeDtypeStruct((strata, items, n_users), BF16)],
        scratch_shapes=[pltpu.VMEM(ratings.shape, BF16), pltpu.SemaphoreType.DMA((strata + 1,))],
        compiler_params=params(44),
        cost_estimate=pl.CostEstimate(flops=0, bytes_accessed=2 * (users.size * 4 + ratings.size * 2), transcendentals=0),
        name="load",
    )(users, ratings)


def grad_kernel(ny, place, stratum, *refs):
    occ, users, rate = refs[:3]
    pieces = refs[3:3 + ny]
    err_hi, err_lo, v_hi, v_lo = refs[3 + ny:7 + ny]
    grads = refs[7 + ny:7 + 2 * ny]
    block, total = refs[7 + 2 * ny:]
    k = lax.axis_index("sub")
    mine = k & (ny - 1)
    chunk = (lax.shift_right_logical(k, ny.bit_length() - 1) + (place + stratum)) & 1
    rows, rank = total.shape
    q = pieces[0].shape[0]
    for r in range(ny):
        block[pl.ds((mine ^ r) * q, q), :] = pieces[r][...]
    v_hi[...], v_lo[...] = split(block[...])
    u = split(users[...])
    pred = dot3((v_hi[...], v_lo[...]), u, ((1,), (1,)))
    at = pl.ds(pl.multiple_of(chunk * rows, TILE), rows)
    err = rate[stratum, at, :].astype(F32) - pred
    parts = []
    for b in range(rows // TILE):
        line = []
        for a in range(err.shape[1] // TILE):
            seen = occ[stratum, chunk * (rows // TILE) + b, a]
            part = err[b * TILE:(b + 1) * TILE, a * TILE:(a + 1) * TILE]
            line.append(jnp.where(seen == 1, part, 0.0))
        parts.append(jnp.concatenate(line, axis=1))
    e = split(jnp.concatenate(parts, axis=0))
    err_hi[...], err_lo[...] = e
    total[...] = dot3(e, u, ((1,), (0,)))
    for r in range(ny):
        grads[r][...] = total[pl.ds((mine ^ r) * q, q), :]


def gradients(occ, users, ratings, pieces, place, stratum):
    ny = len(pieces)
    q, rank = pieces[0].shape
    rows = ny * q
    n_users = users.shape[0]
    return pl.pallas_call(
        functools.partial(grad_kernel, ny, place, stratum),
        in_specs=[SMEM] + [VMEM] * (2 + ny),
        out_specs=[VMEM] * (4 + ny),
        out_shape=[jax.ShapeDtypeStruct((rows, n_users), BF16)] * 2 + [jax.ShapeDtypeStruct((rows, rank), BF16)] * 2
        + [jax.ShapeDtypeStruct((q, rank), F32)] * ny,
        scratch_shapes=[pltpu.VMEM((rows, rank), F32)] * 2,
        compiler_params=params(24),
        cost_estimate=pl.CostEstimate(flops=12 * n_users * rows * rank, bytes_accessed=4 * n_users * rank, transcendentals=0),
        name="gradients",
    )(occ, users, ratings, *pieces)


def step_kernel(n, *refs):
    users, out = refs[0], refs[-1]
    for first in range(0, users.shape[0], BLOCK):
        at = slice(first, first + BLOCK)
        u = users[at, :]
        pull = None
        for i in range(n):
            eh, el, vh, vl = refs[1 + 4 * i:5 + 4 * i]
            part = dot3((eh[:, at], el[:, at]), (vh[...], vl[...]), ((0,), (0,)))
            pull = part if pull is None else pull + part
        out[at, :] = u + 0.02 * (pull - 0.05 * u)


def user_step(users, parts):
    n_users, rank = users.shape
    rows = sum(p[2].shape[0] for p in parts)
    return pl.pallas_call(
        functools.partial(step_kernel, len(parts)),
        in_specs=[VMEM] * (1 + 4 * len(parts)),
        out_specs=VMEM,
        out_shape=jax.ShapeDtypeStruct(users.shape, F32),
        compiler_params=params(24),
        cost_estimate=pl.CostEstimate(flops=6 * n_users * rows * rank, bytes_accessed=8 * n_users * rank, transcendentals=0),
        name="user_step",
    )(users, *[x for p in parts for x in p])


def per_device(n_group, n_sub, users, items, ratings, occupancy):
    strata = ratings.shape[0]
    ny = n_sub // 2
    occupancy = occupancy.transpose(0, 2, 1)

    def over_y(x, r):
        return lax.ppermute(x, "sub", [(i, i ^ r) for i in range(n_sub)])

    def onward(x, r):
        route = []
        for g in range(n_group):
            for i in range(n_sub):
                route.append((g * n_sub + i, (g + 1) % n_group * n_sub + (i ^ r)))
        return lax.ppermute(x, ("group", "sub"), route)

    def gathered(own):
        return [own] + [over_y(own, r) for r in range(1, ny)]

    def arrived(terms):
        return [terms[0]] + [over_y(terms[r], r) for r in range(1, ny)]

    first = gathered(items)
    second = gathered(over_y(items, ny))
    users, ratings = load(users, ratings)
    for s in range(strata):
        last = s == strata - 1
        one = gradients(occupancy, users, ratings, first, 0, s)
        two = gradients(occupancy, users, ratings, second, 1, s)
        base = functools.reduce(jnp.add, arrived(one[4:]))
        base = first[0] + 0.005 * (base - 0.05 * first[0])
        term = functools.reduce(jnp.add, arrived(two[4:]))
        flip = strata % 2 if last else 0
        near = onward(base, 0 if flip else ny) + 0.005 * onward(term, ny if flip else 0)
        if last:
            return user_step(users, [one[:4], two[:4]]), near
        far = onward(base, 0) + 0.005 * onward(term, ny)
        if s == 0:
            users, term = lax.optimization_barrier((users, term))
        else:
            users, base = lax.optimization_barrier((users, base))
        users = user_step(users, [one[:4], two[:4]])
        first, second = gathered(near), gathered(far)


def solution(mesh):
    spec = P(("group", "sub"), None)
    third = P(None, ("group", "sub"), None)
    return jax.shard_map(
        functools.partial(per_device, mesh.shape["group"], mesh.shape["sub"]),
        mesh=mesh,
        in_specs=(spec, spec, third, third),
        out_specs=(spec, spec),
        check_vma=False,
    )
```

```python
import functools

import jax
import jax.numpy as jnp
from jax import lax
from jax.experimental import pallas as pl
from jax.experimental.pallas import tpu as pltpu
from jax.sharding import PartitionSpec as P

TILE = 128
BLOCK = 512
VMEM = pl.BlockSpec(memory_space=pltpu.VMEM)
SMEM = pl.BlockSpec(memory_space=pltpu.SMEM)
F32 = jnp.float32
BF16 = jnp.bfloat16


def split(x):
    hi = x.astype(BF16)
    return hi, (x - hi.astype(F32)).astype(BF16)


def dot3(a, b, dims):
    (ah, al), (bh, bl) = a, b
    dot = functools.partial(lax.dot_general, dimension_numbers=(dims, ((), ())), preferred_element_type=F32)
    return dot(ah, bh) + (dot(ah, bl) + dot(al, bh))


def params(mib):
    return pltpu.CompilerParams(vmem_limit_bytes=mib * 1024 * 1024)


def load_kernel(users, ratings, users_out, turned, held, sems):
    strata = ratings.shape[0]
    copies = [pltpu.make_async_copy(ratings.at[s], held.at[s], sems.at[s]) for s in range(strata)]
    copies.append(pltpu.make_async_copy(users, users_out, sems.at[strata]))
    for copy in copies:
        copy.start()
    for s in range(strata):
        copies[s].wait()
        turned[s] = held[s].T
    copies[strata].wait()


def load(users, ratings):
    strata, n_users, items = ratings.shape
    return pl.pallas_call(
        load_kernel,
        in_specs=[pl.BlockSpec(memory_space=pl.ANY)] * 2,
        out_specs=[VMEM] * 2,
        out_shape=[jax.ShapeDtypeStruct(users.shape, F32), jax.ShapeDtypeStruct((strata, items, n_users), BF16)],
        scratch_shapes=[pltpu.VMEM(ratings.shape, BF16), pltpu.SemaphoreType.DMA((strata + 1,))],
        compiler_params=params(44),
        cost_estimate=pl.CostEstimate(flops=0, bytes_accessed=2 * (users.size * 4 + ratings.size * 2), transcendentals=0),
        name="load",
    )(users, ratings)


def grad_kernel(ny, place, stratum, *refs):
    occ, users, rate = refs[:3]
    pieces = refs[3:3 + ny]
    err_hi, err_lo, v_hi, v_lo = refs[3 + ny:7 + ny]
    grads = refs[7 + ny:7 + 2 * ny]
    block, total = refs[7 + 2 * ny:]
    k = lax.axis_index("sub")
    mine = k & (ny - 1)
    chunk = (lax.shift_right_logical(k, ny.bit_length() - 1) + (place + stratum)) & 1
    rows, rank = total.shape
    q = pieces[0].shape[0]
    for r in range(ny):
        block[pl.ds((mine ^ r) * q, q), :] = pieces[r][...]
    v_hi[...], v_lo[...] = split(block[...])
    u = split(users[...])
    pred = dot3((v_hi[...], v_lo[...]), u, ((1,), (1,)))
    at = pl.ds(pl.multiple_of(chunk * rows, TILE), rows)
    err = rate[stratum, at, :].astype(F32) - pred
    parts = []
    for b in range(rows // TILE):
        line = []
        for a in range(err.shape[1] // TILE):
            seen = occ[stratum, chunk * (rows // TILE) + b, a]
            part = err[b * TILE:(b + 1) * TILE, a * TILE:(a + 1) * TILE]
            line.append(jnp.where(seen == 1, part, 0.0))
        parts.append(jnp.concatenate(line, axis=1))
    e = split(jnp.concatenate(parts, axis=0))
    err_hi[...], err_lo[...] = e
    total[...] = dot3(e, u, ((1,), (0,)))
    for r in range(ny):
        grads[r][...] = total[pl.ds((mine ^ r) * q, q), :]


def gradients(occ, users, ratings, pieces, place, stratum):
    ny = len(pieces)
    q, rank = pieces[0].shape
    rows = ny * q
    n_users = users.shape[0]
    return pl.pallas_call(
        functools.partial(grad_kernel, ny, place, stratum),
        in_specs=[SMEM] + [VMEM] * (2 + ny),
        out_specs=[VMEM] * (4 + ny),
        out_shape=[jax.ShapeDtypeStruct((rows, n_users), BF16)] * 2 + [jax.ShapeDtypeStruct((rows, rank), BF16)] * 2
        + [jax.ShapeDtypeStruct((q, rank), F32)] * ny,
        scratch_shapes=[pltpu.VMEM((rows, rank), F32)] * 2,
        compiler_params=params(24),
        cost_estimate=pl.CostEstimate(flops=12 * n_users * rows * rank, bytes_accessed=4 * n_users * rank, transcendentals=0),
        name="gradients",
    )(occ, users, ratings, *pieces)


def step_kernel(n, *refs):
    users, out = refs[0], refs[-1]
    for first in range(0, users.shape[0], BLOCK):
        at = slice(first, first + BLOCK)
        u = users[at, :]
        pull = None
        for i in range(n):
            eh, el, vh, vl = refs[1 + 4 * i:5 + 4 * i]
            part = dot3((eh[:, at], el[:, at]), (vh[...], vl[...]), ((0,), (0,)))
            pull = part if pull is None else pull + part
        out[at, :] = u + 0.02 * (pull - 0.05 * u)


def user_step(users, parts):
    n_users, rank = users.shape
    rows = sum(p[2].shape[0] for p in parts)
    return pl.pallas_call(
        functools.partial(step_kernel, len(parts)),
        in_specs=[VMEM] * (1 + 4 * len(parts)),
        out_specs=VMEM,
        out_shape=jax.ShapeDtypeStruct(users.shape, F32),
        compiler_params=params(24),
        cost_estimate=pl.CostEstimate(flops=6 * n_users * rows * rank, bytes_accessed=8 * n_users * rank, transcendentals=0),
        name="user_step",
    )(users, *[x for p in parts for x in p])


def per_device(n_group, n_sub, users, items, ratings, occupancy):
    strata = ratings.shape[0]
    ny = n_sub // 2
    occupancy = occupancy.transpose(0, 2, 1)

    def over_y(x, r):
        return lax.ppermute(x, "sub", [(i, i ^ r) for i in range(n_sub)])

    def onward(x, r):
        route = []
        for g in range(n_group):
            for i in range(n_sub):
                route.append((g * n_sub + i, (g + 1) % n_group * n_sub + (i ^ r)))
        return lax.ppermute(x, ("group", "sub"), route)

    def gathered(own):
        return [own] + [over_y(own, r) for r in range(1, ny)]

    def arrived(terms):
        return [terms[0]] + [over_y(terms[r], r) for r in range(1, ny)]

    first = gathered(items)
    second = gathered(over_y(items, ny))
    users, ratings = load(users, ratings)
    for s in range(strata):
        last = s == strata - 1
        one = gradients(occupancy, users, ratings, first, 0, s)
        two = gradients(occupancy, users, ratings, second, 1, s)
        base = functools.reduce(jnp.add, arrived(one[4:]))
        base = first[0] + 0.005 * (base - 0.05 * first[0])
        term = functools.reduce(jnp.add, arrived(two[4:]))
        early = over_y(base, ny)
        rows = early + 0.005 * term
        if last:
            users = user_step(users, [one[:4], two[:4]])
            return users, onward(rows, ny if strata % 2 else 0)
        near = onward(rows, 0)
        far = onward(rows, ny)
        users, base = lax.optimization_barrier((users, base))
        users = user_step(users, [one[:4], two[:4]])
        first = gathered(near)
        second = gathered(far)


def solution(mesh):
    spec = P(("group", "sub"), None)
    third = P(None, ("group", "sub"), None)
    return jax.shard_map(
        functools.partial(per_device, mesh.shape["group"], mesh.shape["sub"]),
        mesh=mesh,
        in_specs=(spec, spec, third, third),
        out_specs=(spec, spec),
        check_vma=False,
    )
```

```python
import functools

import jax
import jax.numpy as jnp
from jax import lax
from jax.experimental import pallas as pl
from jax.experimental.pallas import tpu as pltpu
from jax.sharding import PartitionSpec as P

TILE = 128
BLOCK = 512
VMEM = pl.BlockSpec(memory_space=pltpu.VMEM)
SMEM = pl.BlockSpec(memory_space=pltpu.SMEM)
F32 = jnp.float32
BF16 = jnp.bfloat16


def split(x):
    hi = x.astype(BF16)
    return hi, (x - hi.astype(F32)).astype(BF16)


def dot3(a, b, dims):
    (ah, al), (bh, bl) = a, b
    dot = functools.partial(lax.dot_general, dimension_numbers=(dims, ((), ())), preferred_element_type=F32)
    return dot(ah, bh) + (dot(ah, bl) + dot(al, bh))


def params(mib):
    return pltpu.CompilerParams(vmem_limit_bytes=mib * 1024 * 1024)


def load_kernel(users, ratings, users_out, turned, held, sems):
    strata = ratings.shape[0]
    copies = [pltpu.make_async_copy(ratings.at[s], held.at[s], sems.at[s]) for s in range(strata)]
    copies.append(pltpu.make_async_copy(users, users_out, sems.at[strata]))
    for copy in copies:
        copy.start()
    for s in range(strata):
        copies[s].wait()
        turned[s] = held[s].T
    copies[strata].wait()


def load(users, ratings):
    strata, n_users, items = ratings.shape
    return pl.pallas_call(
        load_kernel,
        in_specs=[pl.BlockSpec(memory_space=pl.ANY)] * 2,
        out_specs=[VMEM] * 2,
        out_shape=[jax.ShapeDtypeStruct(users.shape, F32), jax.ShapeDtypeStruct((strata, items, n_users), BF16)],
        scratch_shapes=[pltpu.VMEM(ratings.shape, BF16), pltpu.SemaphoreType.DMA((strata + 1,))],
        compiler_params=params(44),
        cost_estimate=pl.CostEstimate(flops=0, bytes_accessed=2 * (users.size * 4 + ratings.size * 2), transcendentals=0),
        name="load",
    )(users, ratings)


def grad_kernel(ny, place, stratum, *refs):
    occ, users, rate = refs[:3]
    pieces = refs[3:3 + ny]
    err_hi, err_lo, v_hi, v_lo = refs[3 + ny:7 + ny]
    grads = refs[7 + ny:7 + 2 * ny]
    block, total = refs[7 + 2 * ny:]
    k = lax.axis_index("sub")
    mine = k & (ny - 1)
    chunk = (lax.shift_right_logical(k, ny.bit_length() - 1) + (place + stratum)) & 1
    rows, rank = total.shape
    q = pieces[0].shape[0]
    for r in range(ny):
        block[pl.ds((mine ^ r) * q, q), :] = pieces[r][...]
    v_hi[...], v_lo[...] = split(block[...])
    u = split(users[...])
    pred = dot3((v_hi[...], v_lo[...]), u, ((1,), (1,)))
    at = pl.ds(pl.multiple_of(chunk * rows, TILE), rows)
    err = rate[stratum, at, :].astype(F32) - pred
    parts = []
    for b in range(rows // TILE):
        line = []
        for a in range(err.shape[1] // TILE):
            seen = occ[stratum, chunk * (rows // TILE) + b, a]
            part = err[b * TILE:(b + 1) * TILE, a * TILE:(a + 1) * TILE]
            line.append(jnp.where(seen == 1, part, 0.0))
        parts.append(jnp.concatenate(line, axis=1))
    e = split(jnp.concatenate(parts, axis=0))
    err_hi[...], err_lo[...] = e
    total[...] = dot3(e, u, ((1,), (0,)))
    for r in range(ny):
        grads[r][...] = total[pl.ds((mine ^ r) * q, q), :]


def gradients(occ, users, ratings, pieces, place, stratum):
    ny = len(pieces)
    q, rank = pieces[0].shape
    rows = ny * q
    n_users = users.shape[0]
    return pl.pallas_call(
        functools.partial(grad_kernel, ny, place, stratum),
        in_specs=[SMEM] + [VMEM] * (2 + ny),
        out_specs=[VMEM] * (4 + ny),
        out_shape=[jax.ShapeDtypeStruct((rows, n_users), BF16)] * 2 + [jax.ShapeDtypeStruct((rows, rank), BF16)] * 2
        + [jax.ShapeDtypeStruct((q, rank), F32)] * ny,
        scratch_shapes=[pltpu.VMEM((rows, rank), F32)] * 2,
        compiler_params=params(24),
        cost_estimate=pl.CostEstimate(flops=12 * n_users * rows * rank, bytes_accessed=4 * n_users * rank, transcendentals=0),
        name="gradients",
    )(occ, users, ratings, *pieces)


def step_kernel(n, *refs):
    users, out = refs[0], refs[-1]
    for first in range(0, users.shape[0], BLOCK):
        at = slice(first, first + BLOCK)
        u = users[at, :]
        pull = None
        for i in range(n):
            eh, el, vh, vl = refs[1 + 4 * i:5 + 4 * i]
            part = dot3((eh[:, at], el[:, at]), (vh[...], vl[...]), ((0,), (0,)))
            pull = part if pull is None else pull + part
        out[at, :] = u + 0.02 * (pull - 0.05 * u)


def user_step(users, parts):
    n_users, rank = users.shape
    rows = sum(p[2].shape[0] for p in parts)
    return pl.pallas_call(
        functools.partial(step_kernel, len(parts)),
        in_specs=[VMEM] * (1 + 4 * len(parts)),
        out_specs=VMEM,
        out_shape=jax.ShapeDtypeStruct(users.shape, F32),
        compiler_params=params(24),
        cost_estimate=pl.CostEstimate(flops=6 * n_users * rows * rank, bytes_accessed=8 * n_users * rank, transcendentals=0),
        name="user_step",
    )(users, *[x for p in parts for x in p])


def per_device(n_group, n_sub, users, items, ratings, occupancy):
    strata = ratings.shape[0]
    ny = n_sub // 2
    occupancy = occupancy.transpose(0, 2, 1)

    def over_y(x, r):
        return lax.ppermute(x, "sub", [(i, i ^ r) for i in range(n_sub)])

    def onward(x, r):
        route = []
        for g in range(n_group):
            for i in range(n_sub):
                route.append((g * n_sub + i, (g + 1) % n_group * n_sub + (i ^ r)))
        return lax.ppermute(x, ("group", "sub"), route)

    def gathered(own):
        return [own] + [over_y(own, r) for r in range(1, ny)]

    def arrived(terms):
        return [terms[0]] + [over_y(terms[r], r) for r in range(1, ny)]

    first = gathered(items)
    second = gathered(over_y(items, ny))
    users, ratings = load(users, ratings)
    for s in range(strata):
        last = s == strata - 1
        one = gradients(occupancy, users, ratings, first, 0, s)
        two = gradients(occupancy, users, ratings, second, 1, s)
        base = functools.reduce(jnp.add, arrived(one[4:]))
        base = first[0] + 0.005 * (base - 0.05 * first[0])
        term = functools.reduce(jnp.add, arrived(two[4:]))
        flip = strata % 2 if last else 0
        near = onward(base, 0 if flip else ny)
        late = onward(term, ny if flip else 0)
        near = near + 0.005 * late
        if last:
            return user_step(users, [one[:4], two[:4]]), near
        users, base = lax.optimization_barrier((users, base))
        users = user_step(users, [one[:4], two[:4]])
        far = over_y(near, ny)
        first = gathered(near)
        second = gathered(far)


def solution(mesh):
    spec = P(("group", "sub"), None)
    third = P(None, ("group", "sub"), None)
    return jax.shard_map(
        functools.partial(per_device, mesh.shape["group"], mesh.shape["sub"]),
        mesh=mesh,
        in_specs=(spec, spec, third, third),
        out_specs=(spec, spec),
        check_vma=False,
    )
```

```python
import functools

import jax
import jax.numpy as jnp
from jax import lax
from jax.experimental import pallas as pl
from jax.experimental.pallas import tpu as pltpu
from jax.sharding import PartitionSpec as P

TILE = 128
BLOCK = 512
VMEM = pl.BlockSpec(memory_space=pltpu.VMEM)
SMEM = pl.BlockSpec(memory_space=pltpu.SMEM)
F32 = jnp.float32
BF16 = jnp.bfloat16


def split(x):
    hi = x.astype(BF16)
    return hi, (x - hi.astype(F32)).astype(BF16)


def dot3(a, b, dims):
    (ah, al), (bh, bl) = a, b
    dot = functools.partial(lax.dot_general, dimension_numbers=(dims, ((), ())), preferred_element_type=F32)
    return dot(ah, bh) + (dot(ah, bl) + dot(al, bh))


def params(mib):
    return pltpu.CompilerParams(vmem_limit_bytes=mib * 1024 * 1024)


def load_kernel(users, ratings, users_out, turned, held, sems):
    strata = ratings.shape[0]
    copies = [pltpu.make_async_copy(ratings.at[s], held.at[s], sems.at[s]) for s in range(strata)]
    copies.append(pltpu.make_async_copy(users, users_out, sems.at[strata]))
    for copy in copies:
        copy.start()
    for s in range(strata):
        copies[s].wait()
        turned[s] = held[s].T
    copies[strata].wait()


def load(users, ratings):
    strata, n_users, items = ratings.shape
    return pl.pallas_call(
        load_kernel,
        in_specs=[pl.BlockSpec(memory_space=pl.ANY)] * 2,
        out_specs=[VMEM] * 2,
        out_shape=[jax.ShapeDtypeStruct(users.shape, F32), jax.ShapeDtypeStruct((strata, items, n_users), BF16)],
        scratch_shapes=[pltpu.VMEM(ratings.shape, BF16), pltpu.SemaphoreType.DMA((strata + 1,))],
        compiler_params=params(44),
        cost_estimate=pl.CostEstimate(flops=0, bytes_accessed=2 * (users.size * 4 + ratings.size * 2), transcendentals=0),
        name="load",
    )(users, ratings)


def grad_kernel(ny, place, stratum, *refs):
    occ, users, rate = refs[:3]
    pieces = refs[3:3 + ny]
    err_hi, err_lo, v_hi, v_lo = refs[3 + ny:7 + ny]
    grads = refs[7 + ny:7 + 2 * ny]
    block, total = refs[7 + 2 * ny:]
    k = lax.axis_index("sub")
    mine = k & (ny - 1)
    chunk = (lax.shift_right_logical(k, ny.bit_length() - 1) + (place + stratum)) & 1
    rows, rank = total.shape
    q = pieces[0].shape[0]
    for r in range(ny):
        block[pl.ds((mine ^ r) * q, q), :] = pieces[-r % ny][...]
    v_hi[...], v_lo[...] = split(block[...])
    u = split(users[...])
    pred = dot3((v_hi[...], v_lo[...]), u, ((1,), (1,)))
    at = pl.ds(pl.multiple_of(chunk * rows, TILE), rows)
    err = rate[stratum, at, :].astype(F32) - pred
    parts = []
    for b in range(rows // TILE):
        line = []
        for a in range(err.shape[1] // TILE):
            seen = occ[stratum, chunk * (rows // TILE) + b, a]
            part = err[b * TILE:(b + 1) * TILE, a * TILE:(a + 1) * TILE]
            line.append(jnp.where(seen == 1, part, 0.0))
        parts.append(jnp.concatenate(line, axis=1))
    e = split(jnp.concatenate(parts, axis=0))
    err_hi[...], err_lo[...] = e
    total[...] = dot3(e, u, ((1,), (0,)))
    for r in range(ny):
        grads[r][...] = total[pl.ds((mine ^ r) * q, q), :]


def gradients(occ, users, ratings, pieces, place, stratum):
    ny = len(pieces)
    q, rank = pieces[0].shape
    rows = ny * q
    n_users = users.shape[0]
    return pl.pallas_call(
        functools.partial(grad_kernel, ny, place, stratum),
        in_specs=[SMEM] + [VMEM] * (2 + ny),
        out_specs=[VMEM] * (4 + ny),
        out_shape=[jax.ShapeDtypeStruct((rows, n_users), BF16)] * 2 + [jax.ShapeDtypeStruct((rows, rank), BF16)] * 2
        + [jax.ShapeDtypeStruct((q, rank), F32)] * ny,
        scratch_shapes=[pltpu.VMEM((rows, rank), F32)] * 2,
        compiler_params=params(24),
        cost_estimate=pl.CostEstimate(flops=12 * n_users * rows * rank, bytes_accessed=4 * n_users * rank, transcendentals=0),
        name="gradients",
    )(occ, users, ratings, *pieces)


def step_kernel(n, *refs):
    users, out = refs[0], refs[-1]
    for first in range(0, users.shape[0], BLOCK):
        at = slice(first, first + BLOCK)
        u = users[at, :]
        pull = None
        for i in range(n):
            eh, el, vh, vl = refs[1 + 4 * i:5 + 4 * i]
            part = dot3((eh[:, at], el[:, at]), (vh[...], vl[...]), ((0,), (0,)))
            pull = part if pull is None else pull + part
        out[at, :] = u + 0.02 * (pull - 0.05 * u)


def user_step(users, parts):
    n_users, rank = users.shape
    rows = sum(p[2].shape[0] for p in parts)
    return pl.pallas_call(
        functools.partial(step_kernel, len(parts)),
        in_specs=[VMEM] * (1 + 4 * len(parts)),
        out_specs=VMEM,
        out_shape=jax.ShapeDtypeStruct(users.shape, F32),
        compiler_params=params(24),
        cost_estimate=pl.CostEstimate(flops=6 * n_users * rows * rank, bytes_accessed=8 * n_users * rank, transcendentals=0),
        name="user_step",
    )(users, *[x for p in parts for x in p])


def per_device(n_group, n_sub, users, items, ratings, occupancy):
    strata = ratings.shape[0]
    ny = n_sub // 2
    occupancy = occupancy.transpose(0, 2, 1)

    def over_y(x, r):
        return lax.ppermute(x, "sub", [(i, i ^ r) for i in range(n_sub)])

    def onward(x, r):
        route = []
        for g in range(n_group):
            for i in range(n_sub):
                route.append((g * n_sub + i, (g + 1) % n_group * n_sub + (i ^ r)))
        return lax.ppermute(x, ("group", "sub"), route)

    def gathered(own):
        return [own] + [over_y(own, r) for r in range(ny - 1, 0, -1)]

    def arrived(terms):
        return [terms[0]] + [over_y(terms[r], r) for r in range(1, ny)]

    first = gathered(items)
    second = gathered(over_y(items, ny))
    users, ratings = load(users, ratings)
    for s in range(strata):
        last = s == strata - 1
        one = gradients(occupancy, users, ratings, first, 0, s)
        two = gradients(occupancy, users, ratings, second, 1, s)
        base = functools.reduce(jnp.add, arrived(one[4:]))
        base = first[0] + 0.005 * (base - 0.05 * first[0])
        term = functools.reduce(jnp.add, arrived(two[4:]))
        flip = strata % 2 if last else 0
        near = onward(base, 0 if flip else ny) + 0.005 * onward(term, ny if flip else 0)
        if last:
            return user_step(users, [one[:4], two[:4]]), near
        far = onward(base, 0) + 0.005 * onward(term, ny)
        if s == 0:
            users, term = lax.optimization_barrier((users, term))
        else:
            users, base = lax.optimization_barrier((users, base))
        users = user_step(users, [one[:4], two[:4]])
        first, second = gathered(near), gathered(far)


def solution(mesh):
    spec = P(("group", "sub"), None)
    third = P(None, ("group", "sub"), None)
    return jax.shard_map(
        functools.partial(per_device, mesh.shape["group"], mesh.shape["sub"]),
        mesh=mesh,
        in_specs=(spec, spec, third, third),
        out_specs=(spec, spec),
        check_vma=False,
    )
```

```python
import functools

import jax
import jax.numpy as jnp
from jax import lax
from jax.experimental import pallas as pl
from jax.experimental.pallas import tpu as pltpu
from jax.sharding import PartitionSpec as P

TILE = 128
BLOCK = 512
VMEM = pl.BlockSpec(memory_space=pltpu.VMEM)
SMEM = pl.BlockSpec(memory_space=pltpu.SMEM)
F32 = jnp.float32
BF16 = jnp.bfloat16


def split(x):
    hi = x.astype(BF16)
    return hi, (x - hi.astype(F32)).astype(BF16)


def dot3(a, b, dims):
    (ah, al), (bh, bl) = a, b
    dot = functools.partial(lax.dot_general, dimension_numbers=(dims, ((), ())), preferred_element_type=F32)
    return dot(ah, bh) + (dot(ah, bl) + dot(al, bh))


def params(mib):
    return pltpu.CompilerParams(vmem_limit_bytes=mib * 1024 * 1024)


def load_kernel(users, ratings, users_out, turned, held, sems):
    strata = ratings.shape[0]
    copies = [pltpu.make_async_copy(ratings.at[s], held.at[s], sems.at[s]) for s in range(strata)]
    copies.append(pltpu.make_async_copy(users, users_out, sems.at[strata]))
    for copy in copies:
        copy.start()
    for s in range(strata):
        copies[s].wait()
        turned[s] = held[s].T
    copies[strata].wait()


def load(users, ratings):
    strata, n_users, items = ratings.shape
    return pl.pallas_call(
        load_kernel,
        in_specs=[pl.BlockSpec(memory_space=pl.ANY)] * 2,
        out_specs=[VMEM] * 2,
        out_shape=[jax.ShapeDtypeStruct(users.shape, F32), jax.ShapeDtypeStruct((strata, items, n_users), BF16)],
        scratch_shapes=[pltpu.VMEM(ratings.shape, BF16), pltpu.SemaphoreType.DMA((strata + 1,))],
        compiler_params=params(44),
        cost_estimate=pl.CostEstimate(flops=0, bytes_accessed=2 * (users.size * 4 + ratings.size * 2), transcendentals=0),
        name="load",
    )(users, ratings)


def grad_kernel(ny, place, stratum, *refs):
    occ, users, rate = refs[:3]
    pieces = refs[3:3 + ny]
    err_hi, err_lo, v_hi, v_lo = refs[3 + ny:7 + ny]
    grads = refs[7 + ny:]
    k = lax.axis_index("sub")
    mine = k & (ny - 1)
    chunk = (lax.shift_right_logical(k, ny.bit_length() - 1) + (place + stratum)) & 1
    q = pieces[0].shape[0]
    for r in range(ny):
        at = slice(r * q, r * q + q)
        v_hi[at, :], v_lo[at, :] = split(pieces[-r % ny][...])
    u = split(users[...])
    pred = dot3((v_hi[...], v_lo[...]), u, ((1,), (1,)))
    parts = []
    for r in range(ny):
        row = (chunk * ny + (mine ^ r)) * q
        err = rate[stratum, pl.ds(pl.multiple_of(row, q), q), :].astype(F32) - pred[r * q:r * q + q]
        line = []
        for a in range(err.shape[1] // TILE):
            seen = occ[stratum, lax.div(row, TILE), a]
            line.append(jnp.where(seen == 1, err[:, a * TILE:(a + 1) * TILE], 0.0))
        parts.append(jnp.concatenate(line, axis=1))
    e = split(jnp.concatenate(parts, axis=0))
    err_hi[...], err_lo[...] = e
    term = dot3(e, u, ((1,), (0,)))
    for r in range(ny):
        grads[r][...] = term[r * q:r * q + q]


def gradients(occ, users, ratings, pieces, place, stratum):
    ny = len(pieces)
    q, rank = pieces[0].shape
    rows = ny * q
    n_users = users.shape[0]
    return pl.pallas_call(
        functools.partial(grad_kernel, ny, place, stratum),
        in_specs=[SMEM] + [VMEM] * (2 + ny),
        out_specs=[VMEM] * (4 + ny),
        out_shape=[jax.ShapeDtypeStruct((rows, n_users), BF16)] * 2 + [jax.ShapeDtypeStruct((rows, rank), BF16)] * 2
        + [jax.ShapeDtypeStruct((q, rank), F32)] * ny,
        compiler_params=params(24),
        cost_estimate=pl.CostEstimate(flops=12 * n_users * rows * rank, bytes_accessed=4 * n_users * rank, transcendentals=0),
        name="gradients",
    )(occ, users, ratings, *pieces)


def step_kernel(n, *refs):
    users, out = refs[0], refs[-1]
    for first in range(0, users.shape[0], BLOCK):
        at = slice(first, first + BLOCK)
        u = users[at, :]
        pull = None
        for i in range(n):
            eh, el, vh, vl = refs[1 + 4 * i:5 + 4 * i]
            part = dot3((eh[:, at], el[:, at]), (vh[...], vl[...]), ((0,), (0,)))
            pull = part if pull is None else pull + part
        out[at, :] = u + 0.02 * (pull - 0.05 * u)


def user_step(users, parts):
    n_users, rank = users.shape
    rows = sum(p[2].shape[0] for p in parts)
    return pl.pallas_call(
        functools.partial(step_kernel, len(parts)),
        in_specs=[VMEM] * (1 + 4 * len(parts)),
        out_specs=VMEM,
        out_shape=jax.ShapeDtypeStruct(users.shape, F32),
        compiler_params=params(24),
        cost_estimate=pl.CostEstimate(flops=6 * n_users * rows * rank, bytes_accessed=8 * n_users * rank, transcendentals=0),
        name="user_step",
    )(users, *[x for p in parts for x in p])


def per_device(n_group, n_sub, users, items, ratings, occupancy):
    strata = ratings.shape[0]
    ny = n_sub // 2
    occupancy = occupancy.transpose(0, 2, 1)

    def over_y(x, r):
        return lax.ppermute(x, "sub", [(i, i ^ r) for i in range(n_sub)])

    def onward(x, r):
        route = []
        for g in range(n_group):
            for i in range(n_sub):
                route.append((g * n_sub + i, (g + 1) % n_group * n_sub + (i ^ r)))
        return lax.ppermute(x, ("group", "sub"), route)

    def gathered(own):
        return [own] + [over_y(own, r) for r in range(ny - 1, 0, -1)]

    def arrived(terms):
        return [terms[0]] + [over_y(terms[r], r) for r in range(1, ny)]

    first = gathered(items)
    second = gathered(over_y(items, ny))
    users, ratings = load(users, ratings)
    for s in range(strata):
        last = s == strata - 1
        one = gradients(occupancy, users, ratings, first, 0, s)
        two = gradients(occupancy, users, ratings, second, 1, s)
        base = functools.reduce(jnp.add, arrived(one[4:]))
        base = first[0] + 0.005 * (base - 0.05 * first[0])
        term = functools.reduce(jnp.add, arrived(two[4:]))
        flip = strata % 2 if last else 0
        near = onward(base, 0 if flip else ny) + 0.005 * onward(term, ny if flip else 0)
        if last:
            return user_step(users, [one[:4], two[:4]]), near
        far = onward(base, 0) + 0.005 * onward(term, ny)
        if s == 0:
            users, term = lax.optimization_barrier((users, term))
        else:
            users, base = lax.optimization_barrier((users, base))
        users = user_step(users, [one[:4], two[:4]])
        first, second = gathered(near), gathered(far)


def solution(mesh):
    spec = P(("group", "sub"), None)
    third = P(None, ("group", "sub"), None)
    return jax.shard_map(
        functools.partial(per_device, mesh.shape["group"], mesh.shape["sub"]),
        mesh=mesh,
        in_specs=(spec, spec, third, third),
        out_specs=(spec, spec),
        check_vma=False,
    )
```
